256 devices in a mesh: px: 16 (over x, z_hi, core), py: 16 (over y, z_lo).
Axes of the slice: x: 4, y: 4, z: 8 (z_hi: 2, z_lo: 4; z = z_hi * 4 + z_lo), core: 2. Of those that a mesh axis runs over, the one named last changes fastest.
Arguments:
- fluid: float32 [3, 512, 32, 2048], P(None, 'px', 'py'), may hold values from -6 to 6
- part_vel: float32 [3, 64, 64, 1024], P(None, 'px', 'py'), may hold values from -6 to 6
- part_frac: float32 [3, 64, 64, 1024], P(None, 'px', 'py'), may hold values from -0.5 to 0.5
- stokes_time: float32 [64, 64, 1024], P('px', 'py'), may hold values from 0.5 to 5
- cells: int32 [64, 64, 1024], P('px', 'py'), may hold values from 0 to 8191
- counts: int32 [64, 64], P('px', 'py'), may hold values from 96 to 1024, as said below
Outputs:
- fluid_next: float32 [3, 512, 32, 2048], P(None, 'px', 'py')
- vel_next: float32 [3, 64, 64, 1024], P(None, 'px', 'py')
The draws below stay inside these ranges and needn't reach their ends.
Inputs may be any that keep to these rules, and one draw needn't show every extreme that they name: cells = (ix * 32 + iy) * 32 + iz with ix, iy, iz the particle's cell in its sub-brick of 8 x 32 x 32 cells. Slots 0 to counts - 1 of a sub-brick hold live particles, the others are padding; some sub-brick is full.
All inputs are finite; a program needn't handle non-finite values.
Results may differ from the reference program's by a relative error of at most 0.0011.
Values may be sent and summed in bfloat16 or wider, within the bound.
No kernel may reach another device: no remote copies, remote signals or barrier semaphores. Data moves between devices by JAX's collectives and lax.ppermute only.
A program may use at most 64 MiB of HBM per device.

```python
import math
import jax
import jax.numpy as jnp
from jax import lax

SX = 8
SY = 32
NY = 2048
CAP = 1024
NX = 512
NZ = 32
NXS = 64
NYS = 64
SUB_X = 4
SUB_Y = 4


def draw_fluid(key, part):
    key = jax.random.fold_in(key, 11)
    return jnp.clip(jax.random.normal(key, (3, NX, NZ, NY), jnp.float32), -6.0, 6.0)


def draw_counts(key, part):
    key = jax.random.fold_in(key, 5)
    level_key, jitter_key, pick_key = jax.random.split(key, 3)
    rows = NXS // SUB_X
    columns = NYS // SUB_Y
    levels = jax.random.randint(level_key, (rows, columns), 0, 4)
    picked = jax.random.randint(pick_key, (), 0, rows * columns)
    chosen = jnp.arange(rows * columns).reshape(rows, columns) == picked
    levels = jnp.where(chosen, 0, levels)
    levels = jnp.repeat(jnp.repeat(levels, SUB_X, axis=0), SUB_Y, axis=1)
    chosen = jnp.repeat(jnp.repeat(chosen, SUB_X, axis=0), SUB_Y, axis=1)
    highest = CAP // jnp.left_shift(jnp.ones_like(levels), levels)
    jitter = jax.random.randint(jitter_key, (NXS, NYS), 0, 1 << 30) % (highest // 4 + 1)
    jitter = jnp.where(chosen, 0, jitter)
    return (highest - jitter).astype(jnp.int32)


def plant(array, own_key, smallest, top_value):
    longest = array.shape.index(max(array.shape))
    spots = []
    for shift in (0, 1):
        where = [jax.random.randint(jax.random.fold_in(own_key, axis), (), 0, length) for axis, length in enumerate(array.shape)]
        where[longest] = (where[longest] + shift) % array.shape[longest]
        spots.append(tuple(where))
    return array.at[spots[0]].set(smallest).at[spots[1]].set(top_value)


def shard_levels(rng, extent, shards, least, largest):
    level = 1.0
    for axis_at, shards_of in shards:
        heights = jax.random.uniform(jax.random.fold_in(jax.random.fold_in(rng, 6), axis_at), (shards_of,), jnp.float32, least / len(shards), largest / len(shards))
        level = level * jnp.repeat(jnp.exp(heights), extent[axis_at] // shards_of).reshape((-1,) + (1,) * (len(extent) - 1 - axis_at))
    return level


def normal_values(key, dims, scale, most, shards=(), kind=jnp.bfloat16):
    entries = jax.random.normal(key, dims, jnp.float32) * scale
    if len(shards) > 0:
        entries = shard_levels(key, dims, shards, -0.22, 0.18) * entries
    return jnp.clip(entries, min=-most, max=most).astype(kind)


def setup_inputs(seed: int = 0) -> dict:
    keys = jax.random.split(jax.random.key(seed), 7)
    return {
        "fluid": draw_fluid(jax.random.fold_in(keys[6], 71), 0),
        "part_vel": normal_values(keys[1], (3, NXS, NYS, CAP), 1.0, 6.0, ((1, 16), (2, 16)), jnp.float32),
        "part_frac": jnp.clip(jax.random.uniform(keys[2], (3, NXS, NYS, CAP), jnp.float32, -0.5, 0.5) * shard_levels(keys[2], (3, NXS, NYS, CAP), ((1, 16), (2, 16)), -0.4, 0.0), -0.5, 0.5),
        "stokes_time": jnp.clip(jnp.exp(math.log(5.0) - 2.3025851 * jax.random.uniform(keys[3], (NXS, NYS, CAP), jnp.float32) ** shard_levels(keys[3], (NXS, NYS, CAP), ((0, 16), (1, 16)), -0.2, 0.2)), 0.5, 5.0),
        "cells": plant(jax.random.randint(keys[4], (NXS, NYS, CAP), 0, SX * SY * NZ), jax.random.fold_in(keys[4], 1), 0, (SX * SY * NZ) - 1).astype(jnp.int32),
        "counts": draw_counts(jax.random.fold_in(keys[6], 71), 0),
    }


mass_load = 4.0
step_dt = 0.5
viscous_step = 0.25
forcing_gain = 1.5
forced_modes = 4.0


def cloud_weights(offsets):
    return jnp.stack([0.5 * (0.5 - offsets) ** 2, 0.75 - offsets * offsets, 0.5 * (0.5 + offsets) ** 2])


def mode_gain(wavenum, length):
    wave_angle = 2.0 * math.pi * wavenum / length
    damping = jnp.exp(-viscous_step * wave_angle * wave_angle)
    boosted = jnp.where((wavenum >= 1.0) & (wavenum <= forced_modes), 1.0 + forcing_gain, 1.0)
    return damping * boosted


def reference(fluid, part_vel, part_frac, stokes_time, cells, counts):
    field = lax.optimization_barrier(fluid.astype(jnp.bfloat16))
    slot_ids = jnp.arange(CAP, dtype=jnp.int32)
    tile_ids = jnp.arange(NYS, dtype=jnp.int32)

    def row_step(deposit, inputs):
        row_id, velocity, offsets, response, cell_ids, filled = inputs
        x_cell = cell_ids // (SY * NZ)
        y_cell = (cell_ids // NZ) % SY
        z_cell = cell_ids % NZ
        x_base = row_id * SX + x_cell
        y_base = tile_ids[:, None] * SY + y_cell
        present = slot_ids[None, :] < filled[:, None]
        weight_x = cloud_weights(offsets[0])
        masked_y = jnp.where(present[None], cloud_weights(offsets[1]), 0.0)
        weight_y = lax.optimization_barrier(masked_y.astype(jnp.bfloat16)).astype(jnp.float32)
        weight_z = cloud_weights(offsets[2])
        interp = jnp.zeros(velocity.shape, jnp.float32)
        for step_x in range(3):
            for step_y in range(3):
                for step_z in range(3):
                    x_rows = (x_base + step_x - 1) % NX
                    z_rows = (z_cell + step_z - 1) % NZ
                    y_rows = (y_base + step_y - 1) % NY
                    values = field[:, x_rows, z_rows, y_rows].astype(jnp.float32)
                    interp = interp + weight_x[step_x] * weight_z[step_z] * (weight_y[step_y] * values)
        drag_rate = step_dt / response
        slip_vel = interp - velocity
        vel_next = jnp.where(present[None], velocity + drag_rate * slip_vel, velocity)
        source = jnp.where(present[None], -mass_load * drag_rate * slip_vel, 0.0)
        for step_x in range(3):
            for step_z in range(3):
                share = source * weight_x[step_x] * weight_z[step_z]
                share = lax.optimization_barrier(share.astype(jnp.bfloat16)).astype(jnp.float32)
                for step_y in range(3):
                    x_rows = (x_base + step_x - 1) % NX
                    z_rows = (z_cell + step_z - 1) % NZ
                    y_rows = (y_base + step_y - 1) % NY
                    deposit = deposit.at[:, x_rows, z_rows, y_rows].add(share * weight_y[step_y])
        return deposit, vel_next

    inputs = (jnp.arange(NXS, dtype=jnp.int32), jnp.transpose(part_vel, (1, 0, 2, 3)),
              jnp.transpose(part_frac, (1, 0, 2, 3)), stokes_time, cells, counts)
    deposit, vel_rows = lax.scan(row_step, jnp.zeros(fluid.shape, jnp.float32), inputs)
    vel_next = jnp.transpose(vel_rows, (1, 0, 2, 3))
    low_deposit = lax.optimization_barrier(deposit.astype(jnp.bfloat16)).astype(jnp.float32)
    mixed = fluid + low_deposit
    wavenum = jnp.arange(NY // 2 + 1).astype(jnp.float32)
    spectrum = jnp.fft.rfft(mixed, axis=-1) * mode_gain(wavenum, NY)
    fluid_next = jnp.fft.irfft(spectrum, n=NY, axis=-1).astype(jnp.float32)
    return fluid_next, vel_next
```

```python
import functools
import math

import jax
import jax.numpy as jnp
import numpy as np
from jax import lax
from jax.experimental import pallas as pl
from jax.experimental.pallas import tpu as pltpu
from jax.sharding import PartitionSpec as P

mass_load = 4.0
step_dt = 0.5
viscous_step = 0.25
forcing_gain = 1.5
forced_modes = 4

COMPS = 3
LANES = 128
VMEM_LIMIT = 32 * 1024 * 1024
f32 = jnp.float32
bf16 = jnp.bfloat16
NT = (((1,), (1,)), ((), ()))


def filter_blocks(length, width):
    k = np.fft.fftfreq(length, 1.0 / length)
    angle = 2.0 * math.pi * k / length
    gain = np.exp(-viscous_step * angle * angle)
    gain = gain * np.where((abs(k) >= 1) & (abs(k) <= forced_modes), 1.0 + forcing_gain, 1.0)
    taps = np.fft.ifft(gain).real
    blocks = length // width
    half = blocks // 2
    inner = np.arange(width)
    full = []
    for d in range(blocks):
        full.append(taps[(width * d + inner[None, :] - inner[:, None]) % length])
    sums = np.stack([0.5 * (full[d] + full[d + half]) for d in range(half)])
    diffs = np.stack([0.5 * (full[d] - full[d + half]) for d in range(half)])
    both = np.stack([sums, diffs]).astype(np.float32)
    high = both.astype(jnp.bfloat16)
    low = (both - high.astype(np.float32)).astype(jnp.bfloat16)
    return high, low


def pack_kernel(dims, grid_ref, before_ref, after_ref, out_ref, msg):
    width, devices, planes = dims
    span = width + 2
    rows = COMPS * span
    used = planes * rows
    total = out_ref.shape[1]
    for j in range(devices):
        base = j * total
        msg[pl.ds(base + used, total - used), :] = jnp.zeros((total - used, LANES), f32)
        for p in range(planes):
            for c in range(COMPS):
                at = base + p * rows + c * span
                e = p * COMPS + c
                lanes = slice(j * LANES, (j + 1) * LANES)
                msg[pl.ds(at, 1), :] = before_ref[e : e + 1, lanes].astype(f32)
                msg[pl.ds(at + 1, width), :] = grid_ref[
                    pl.ds(c * width * devices * planes + j * planes + p, width, stride=devices * planes), :
                ]
                msg[pl.ds(at + 1 + width, 1), :] = after_ref[e : e + 1, lanes].astype(f32)
    row_id = lax.broadcasted_iota(jnp.int32, (8, LANES), 0)
    lane_id = lax.broadcasted_iota(jnp.int32, (8, LANES), 1)
    pick = ((row_id == 0) & (lane_id == LANES - 1)) | ((row_id == 1) & (lane_id == 0))
    pick = jnp.where(pick, 1.0, 0.0).astype(bf16)
    for j in range(devices):
        for p in range(planes):
            block = msg[pl.ds(j * total + p * rows, rows), :].astype(bf16)
            edge = lax.dot_general(pick, block, NT, preferred_element_type=f32)
            right = (j + 1) % devices
            left = (j - 1) % devices
            msg[pl.ds(right * total + used + 2 * p, 1), 0:rows] = edge[0:1]
            msg[pl.ds(left * total + used + 2 * p + 1, 1), 0:rows] = edge[1:2]
    for j in range(devices):
        out_ref[j] = msg[pl.ds(j * total, total), :].astype(bf16)


def same_cell(c, span, depth, rows):
    row = lax.broadcasted_iota(jnp.int32, (rows, LANES), 0)
    col = lax.broadcasted_iota(jnp.int32, (rows, LANES), 1)
    return jnp.where(row // depth == col - c * span, 1.0, 0.0).astype(bf16)


def side_lane(depth, shape, dim):
    ghost = lax.broadcasted_iota(jnp.int32, shape, dim)
    lane = lax.broadcasted_iota(jnp.int32, shape, 1 - dim)
    hit = ((ghost < depth) & (lane == LANES - 1)) | ((ghost >= depth) & (lane == 0))
    return jnp.where(hit, 1.0, 0.0).astype(bf16)


def particle_kernel(
    dims, counts_ref, recv_ref, vel_ref, frac_ref, tau_ref, cells_ref,
    vel_out_ref, send_ref, msg, rows_buf, ghost, field, deposit, prep, ints,
):
    width, devices, planes, subs_x, subs_y, slots, chunk = dims
    span = width + 2
    depth = devices * planes
    tile_x = width // subs_x
    tile_y = LANES // subs_y
    total = recv_ref.shape[1]
    rows = COMPS * span
    used = planes * rows
    cells = span * depth
    near = 4
    pair = 2 * depth
    pairs = tile_x // 2
    core = cells - pair
    block = near * depth

    for s in range(devices):
        msg[...] = recv_ref[s].astype(f32)
        for p in range(planes):
            z = s * planes + p
            for c in range(COMPS):
                rows_buf[pl.ds(c * cells + z, span, stride=depth), :] = msg[
                    pl.ds(p * rows + c * span, span), :
                ]
            ghost[pl.ds(z, 1), :] = msg[pl.ds(used + 2 * p, 1), :]
            ghost[pl.ds(depth + z, 1), :] = msg[pl.ds(used + 2 * p + 1, 1), :]
    own_z = lax.broadcasted_iota(jnp.int32, (cells, 2 * depth), 0) % depth
    own_z = own_z == lax.broadcasted_iota(jnp.int32, (cells, 2 * depth), 1) % depth
    lane = lax.broadcasted_iota(jnp.int32, (cells, LANES), 1)
    for c in range(COMPS):
        at = pl.ds(c * cells, cells)
        wide = lax.dot_general(
            same_cell(c, span, depth, cells), ghost[...].astype(bf16), NT, preferred_element_type=f32
        )
        wide = jnp.where(own_z, wide, 0.0).astype(bf16)
        outer = jnp.dot(wide, side_lane(depth, (2 * depth, LANES), 0), preferred_element_type=f32)
        inner = rows_buf[at, :]
        lower = jnp.where(lane == LANES - 1, outer, inner)
        upper = jnp.where(lane == 0, outer, inner)
        core = cells - pair
        lane_id = lane[:core]
        for b in range(subs_y):
            value = lower if 2 * b < subs_y else upper
            moved = jnp.roll(value[pair:], LANES // 2, axis=1)
            first_half = (lane_id - (b * tile_y - 16)) % LANES < LANES // 2
            field[b, pl.ds(c * core, core), :] = jnp.where(first_half, value[:core], moved).astype(bf16)

    x_rows = lax.broadcasted_iota(jnp.int32, (8, chunk), 0)
    z_rows = lax.broadcasted_iota(jnp.int32, (depth, chunk), 0)
    y_rows = lax.broadcasted_iota(jnp.int32, (tile_y + 16, chunk), 0) - 8

    def strip(a, carry):
        for d in range(COMPS):
            f = frac_ref[d, a]
            prep[3 * d] = 0.5 * (0.5 - f) ** 2
            prep[3 * d + 1] = 0.75 - f * f
            prep[3 * d + 2] = 0.5 * (0.5 + f) ** 2
        prep[9] = step_dt / tau_ref[a]
        cell = cells_ref[a]
        ints[0] = cell // (tile_y * depth)
        ints[1] = cell // depth % tile_y
        ints[2] = cell % depth
        first = a * (tile_x * depth)

        for b in range(subs_y):
            filled = counts_ref[a, b]
            blocks = tile_x * depth // block
            data = jnp.concatenate(
                [
                    jnp.concatenate(
                        [
                            field[b, pl.ds(pl.multiple_of(c * core + first + t * block, block), block), :]
                            for t in range(blocks)
                        ],
                        axis=1,
                    )
                    for c in range(COMPS)
                ],
                axis=0,
            )
            acc = None
            for start in range(0, slots, chunk):
                at = slice(start, start + chunk)
                row = lambda i: prep[i, b : b + 1, at]
                xc, yc, zc = (ints[i, b : b + 1, at] for i in range(3))
                here = lax.broadcasted_iota(jnp.int32, (1, chunk), 1) + start < filled
                dx = x_rows - (xc & 1)
                wx = jnp.where(
                    dx == 0, row(0), jnp.where(dx == 1, row(1), jnp.where(dx == 2, row(2), 0.0))
                )
                dy = y_rows - yc
                y_low, y_mid, y_high = (jnp.where(here, row(3 + i), 0.0) for i in range(3))
                wy = jnp.where(
                    dy == -1, y_low, jnp.where(dy == 0, y_mid, jnp.where(dy == 1, y_high, 0.0))
                )
                dz = (z_rows - zc + 1) & (depth - 1)
                wz = jnp.where(
                    dz == 0, row(6), jnp.where(dz == 1, row(7), jnp.where(dz == 2, row(8), 0.0))
                )
                groups = LANES // 8
                half_groups = groups // 2
                blank = jnp.zeros((8, chunk), f32)
                pieces = [blank] * (groups * blocks)
                for k in range(pairs):
                    chosen = xc >> 1 == k
                    for g in range(tile_y // 8 + 2):
                        place = (b * tile_y // 8 - 1 + g + (k % 2) * half_groups) % groups
                        pieces[k // 2 * groups + place] = jnp.where(chosen, wy[8 * g : 8 * g + 8], 0.0)
                wy = jnp.concatenate(pieces, axis=0).astype(bf16)
                raw = jnp.dot(data, wy, preferred_element_type=f32)
                rate = row(9)
                shares = []
                for c in range(COMPS):
                    found = None
                    for i in range(near):
                        part = None
                        for g in range(depth // 8):
                            at8 = c * block + i * depth + 8 * g
                            term = raw[at8 : at8 + 8] * wz[8 * g : 8 * g + 8]
                            part = term if part is None else part + term
                        part = part * wx[i : i + 1]
                        found = part if found is None else found + part
                    interp = jnp.sum(found, axis=0, keepdims=True)
                    velocity = vel_ref[c, a, b : b + 1, at]
                    change = rate * (interp - velocity)
                    vel_out_ref[c, a, b : b + 1, at] = jnp.where(here, velocity + change, velocity)
                    pull = jnp.where(here, -mass_load * change, 0.0) * wx
                    shares = shares + [(pull[i : i + 1] * wz).astype(bf16) for i in range(near)]
                part = lax.dot_general(
                    jnp.concatenate(shares, axis=0), wy, NT, preferred_element_type=f32
                )
                acc = part if acc is None else acc + part
            for c in range(COMPS):
                for t in range(blocks):
                    base = pl.multiple_of(c * core + first + t * block, block)
                    deposit[b, pl.ds(base, block), :] = acc[
                        c * block : (c + 1) * block, t * LANES : (t + 1) * LANES
                    ]
        return carry

    lax.fori_loop(0, subs_x, strip, 0)

    gathered = jnp.zeros((2 * depth, LANES), f32)
    for c in range(COMPS):
        at = pl.ds(c * cells, cells)
        sides = []
        lane_id = lane[:core]
        empty = jnp.zeros((pair, LANES), f32)
        for side in range(2):
            even = odd = None
            for b in range(side * subs_y // 2, (side + 1) * subs_y // 2):
                value = deposit[b, pl.ds(c * core, core), :]
                first_half = (lane_id - (b * tile_y - 16)) % LANES < LANES // 2
                one = jnp.where(first_half, value, 0.0)
                two = jnp.where(first_half, 0.0, value)
                even = one if even is None else even + one
                odd = two if odd is None else odd + two
            moved = jnp.roll(odd, LANES // 2, axis=1)
            sides.append(
                jnp.concatenate([even, empty], axis=0) + jnp.concatenate([empty, moved], axis=0)
            )
        lower, upper = sides
        first_lane = lane == 0
        last_lane = lane == LANES - 1
        rows_buf[at, :] = jnp.where(last_lane, 0.0, lower) + jnp.where(first_lane, 0.0, upper)
        outer = jnp.where(last_lane, lower, jnp.where(first_lane, upper, 0.0)).astype(bf16)
        wide = jnp.dot(outer, side_lane(depth, (LANES, 2 * depth), 1), preferred_element_type=f32)
        wide = jnp.where(own_z, wide, 0.0).astype(bf16)
        gathered = gathered + lax.dot_general(
            wide, same_cell(c, span, depth, cells), (((0,), (0,)), ((), ())), preferred_element_type=f32
        )
    ghost[...] = gathered
    for s in range(devices):
        for p in range(planes):
            z = s * planes + p
            for c in range(COMPS):
                msg[pl.ds(p * rows + c * span, span), :] = rows_buf[
                    pl.ds(c * cells + z, span, stride=depth), :
                ]
            msg[pl.ds(used + 2 * p, 1), :] = ghost[pl.ds(z, 1), :]
            msg[pl.ds(used + 2 * p + 1, 1), :] = ghost[pl.ds(depth + z, 1), :]
        send_ref[s] = msg[...].astype(bf16)


def particle_call(dims, counts, recv, part_vel, part_frac, stokes_time, cells):
    width, devices, planes, subs_x, subs_y, slots, chunk = dims
    vmem = pl.BlockSpec(memory_space=pltpu.VMEM)
    total = recv.shape[1]
    depth = devices * planes
    all_rows = COMPS * (width + 2) * depth
    core_rows = COMPS * width * depth
    return pl.pallas_call(
        functools.partial(particle_kernel, dims),
        out_shape=(jax.ShapeDtypeStruct(part_vel.shape, f32), jax.ShapeDtypeStruct(recv.shape, bf16)),
        in_specs=[pl.BlockSpec(memory_space=pltpu.SMEM)] + [vmem] * 5,
        out_specs=(vmem, vmem),
        scratch_shapes=[
            pltpu.VMEM((total, LANES), f32),
            pltpu.VMEM((all_rows, LANES), f32),
            pltpu.VMEM((2 * depth, LANES), f32),
            pltpu.VMEM((subs_y, core_rows, LANES), bf16),
            pltpu.VMEM((subs_y, core_rows, LANES), f32),
            pltpu.VMEM((10, subs_y, slots), f32),
            pltpu.VMEM((3, subs_y, slots), jnp.int32),
        ],
        compiler_params=pltpu.CompilerParams(vmem_limit_bytes=VMEM_LIMIT),
        name="particles",
    )(counts, recv, part_vel, part_frac, stokes_time, cells)


def gather_kernel(dims, recv_ref, out_ref, low_ref, high_ref, msg):
    width, devices, planes = dims
    span = width + 2
    rows = COMPS * span
    used = planes * rows
    total = recv_ref.shape[1]
    count = devices
    for j in range(count):
        msg[j] = recv_ref[j].astype(f32)
    side = lax.broadcasted_iota(jnp.int32, (8, LANES), 0)
    lane = lax.broadcasted_iota(jnp.int32, (8, LANES), 1)
    place = ((side == 0) & (lane == LANES - 1)) | ((side == 1) & (lane == 0))
    place = jnp.where(place, 1.0, 0.0).astype(bf16)
    for j in range(count):
        left = (j - 1) % count
        right = (j + 1) % count
        lanes = slice(j * LANES, (j + 1) * LANES)
        lows, highs = [], []
        for p in range(planes):
            pair = jnp.concatenate(
                [
                    msg[right, used + 2 * p : used + 2 * p + 1, :],
                    msg[left, used + 2 * p + 1 : used + 2 * p + 2, :],
                    jnp.zeros((6, LANES), f32),
                ],
                axis=0,
            ).astype(bf16)
            added = lax.dot_general(
                pair, place, (((0,), (0,)), ((), ())), preferred_element_type=f32
            )
            block = msg[j, p * rows : (p + 1) * rows, :] + added[:rows]
            for c in range(COMPS):
                e = p * COMPS + c
                at = c * span
                lows.append(block[at : at + 1])
                highs.append(block[at + span - 1 : at + span])
                out_ref[pl.ds(e * width, width), lanes] = block[at + 1 : at + 1 + width]
        low_ref[:, lanes] = jnp.concatenate(lows, axis=0).astype(bf16)
        high_ref[:, lanes] = jnp.concatenate(highs, axis=0).astype(bf16)


def filter_kernel(dims, grid_ref, dep_ref, from_low_ref, from_high_ref, high_ref, low_ref, out_ref, mixed):
    width, devices, planes = dims
    depth = devices * planes
    for j in range(devices):
        lanes = slice(j * LANES, (j + 1) * LANES)
        for p in range(planes):
            for c in range(COMPS):
                e = p * COMPS + c
                dep = dep_ref[pl.ds(e * width, width), lanes]
                first = dep[:1] + from_low_ref[e : e + 1, lanes].astype(f32)
                last = dep[width - 1 :] + from_high_ref[e : e + 1, lanes].astype(f32)
                dep = jnp.concatenate([first, dep[1 : width - 1], last], axis=0)
                fluid = grid_ref[pl.ds(c * width * depth + j * planes + p, width, stride=depth), :]
                mixed[pl.ds(e * width, width), lanes] = fluid + dep.astype(bf16).astype(f32)
    folds = high_ref.shape[1]
    block = high_ref.shape[2]
    sides = []
    for sign in range(2):
        highs, lows = [], []
        for i in range(folds):
            one = mixed[:, i * block : (i + 1) * block]
            two = mixed[:, (i + folds) * block : (i + folds + 1) * block]
            value = one + two if sign == 0 else one - two
            high = value.astype(bf16)
            highs.append(high)
            lows.append((value - high.astype(f32)).astype(bf16))
        sides.append((highs, lows))
    for o in range(folds):
        results = []
        for sign in range(2):
            highs, lows = sides[sign]
            sums = {1: None, -1: None}
            for i in range(folds):
                d = (o - i) % folds
                key = -1 if sign == 1 and o < i else 1
                part = jnp.dot(highs[i], high_ref[sign, d], preferred_element_type=f32)
                part = part + jnp.dot(lows[i], high_ref[sign, d], preferred_element_type=f32)
                part = part + jnp.dot(highs[i], low_ref[sign, d], preferred_element_type=f32)
                sums[key] = part if sums[key] is None else sums[key] + part
            results.append(sums[1] if sums[-1] is None else sums[1] - sums[-1])
        for flip in range(2):
            value = results[0] + results[1] if flip == 0 else results[0] - results[1]
            for half in range(block // LANES):
                j = (o + flip * folds) * (block // LANES) + half
                for p in range(planes):
                    for c in range(COMPS):
                        e = p * COMPS + c
                        out_ref[pl.ds(c * width * depth + j * planes + p, width, stride=depth), :] = value[
                            e * width : (e + 1) * width, half * LANES : (half + 1) * LANES
                        ]


def per_device(fluid, part_vel, part_frac, stokes_time, cells, counts):
    devices = lax.axis_size("py")
    rows_px = lax.axis_size("px")
    _, width, planes, length = fluid.shape
    subs_x, subs_y, slots = stokes_time.shape
    depth = planes * devices
    span = width + 2
    used = planes * COMPS * span
    total = -(-(used + 2 * planes) // 16) * 16
    up = [(i, (i + 1) % rows_px) for i in range(rows_px)]
    down = [(j, i) for i, j in up]
    params = pltpu.CompilerParams(vmem_limit_bytes=VMEM_LIMIT)
    vmem = pl.BlockSpec(memory_space=pltpu.VMEM)

    edges = jnp.stack([fluid[:, 0], fluid[:, width - 1]])
    edges = edges.transpose(0, 2, 1, 3).reshape(2, planes * COMPS, length).astype(bf16)
    before = lax.ppermute(edges[1], "px", up)
    after = lax.ppermute(edges[0], "px", down)
    grid = fluid.reshape(COMPS * width, planes, devices, LANES).transpose(0, 2, 1, 3)
    grid = grid.reshape(COMPS * width * depth, LANES)
    dims = (width, devices, planes)
    send = pl.pallas_call(
        functools.partial(pack_kernel, dims),
        out_shape=jax.ShapeDtypeStruct((devices, total, LANES), bf16),
        in_specs=[vmem] * 3,
        out_specs=vmem,
        scratch_shapes=[pltpu.VMEM((devices * total, LANES), f32)],
        compiler_params=params,
        name="pack",
    )(grid, before, after)
    recv = lax.all_to_all(send, "py", 0, 0, tiled=True)

    chunk = min(256, slots)
    vel_next, back = particle_call(
        (width, devices, planes, subs_x, subs_y, slots, chunk),
        counts, recv, part_vel, part_frac, stokes_time, cells,
    )
    pencil = lax.all_to_all(back, "py", 0, 0, tiled=True)

    dep, low, high = pl.pallas_call(
        functools.partial(gather_kernel, dims),
        out_shape=(
            jax.ShapeDtypeStruct((planes * COMPS * width, length), f32),
            jax.ShapeDtypeStruct((planes * COMPS, length), bf16),
            jax.ShapeDtypeStruct((planes * COMPS, length), bf16),
        ),
        in_specs=[vmem],
        out_specs=(vmem,) * 3,
        scratch_shapes=[pltpu.VMEM((devices, total, LANES), f32)],
        compiler_params=params,
        name="gather",
    )(pencil)
    from_low = lax.ppermute(high, "px", up)
    from_high = lax.ppermute(low, "px", down)
    taps_high, taps_low = filter_blocks(length, 256)
    out = pl.pallas_call(
        functools.partial(filter_kernel, dims),
        out_shape=jax.ShapeDtypeStruct(grid.shape, f32),
        in_specs=[vmem] * 6,
        out_specs=vmem,
        scratch_shapes=[pltpu.VMEM((planes * COMPS * width, length), f32)],
        compiler_params=params,
        name="filter",
    )(grid, dep, from_low, from_high, jnp.asarray(taps_high), jnp.asarray(taps_low))
    out = out.reshape(COMPS * width, devices, planes, LANES).transpose(0, 2, 1, 3)
    return out.reshape(fluid.shape), vel_next


def solution(mesh):
    placed = (
        P(None, "px", "py", None),
        P(None, "px", "py", None),
        P(None, "px", "py", None),
        P("px", "py", None),
        P("px", "py", None),
        P("px", "py"),
    )
    return jax.shard_map(
        per_device,
        mesh=mesh,
        in_specs=placed,
        out_specs=(P(None, "px", "py", None), P(None, "px", "py", None)),
        check_vma=False,
    )
```

```python
import functools
import math

import jax
import jax.numpy as jnp
import numpy as np
from jax import lax
from jax.experimental import pallas as pl
from jax.experimental.pallas import tpu as pltpu
from jax.sharding import PartitionSpec as P

mass_load = 4.0
step_dt = 0.5
viscous_step = 0.25
forcing_gain = 1.5
forced_modes = 4

COMPS = 3
LANES = 128
VMEM_LIMIT = 24 * 1024 * 1024
VMEM_MOST = 58 * 1024 * 1024
f32 = jnp.float32
bf16 = jnp.bfloat16
NT = (((1,), (1,)), ((), ()))


def filter_blocks(length, width):
    k = np.fft.fftfreq(length, 1.0 / length)
    angle = 2.0 * math.pi * k / length
    gain = np.exp(-viscous_step * angle * angle)
    gain = gain * np.where((abs(k) >= 1) & (abs(k) <= forced_modes), 1.0 + forcing_gain, 1.0)
    taps = np.fft.ifft(gain).real
    blocks = length // width
    half = blocks // 2
    inner = np.arange(width)
    full = []
    for d in range(blocks):
        full.append(taps[(width * d + inner[None, :] - inner[:, None]) % length])
    sums = np.stack([0.5 * (full[d] + full[d + half]) for d in range(half)])
    diffs = np.stack([0.5 * (full[d] - full[d + half]) for d in range(half)])
    both = np.stack([sums, diffs]).astype(np.float32)
    high = both.astype(jnp.bfloat16)
    low = (both - high.astype(np.float32)).astype(jnp.bfloat16)
    return high, low


def side_picker():
    row_id = lax.broadcasted_iota(jnp.int32, (8, LANES), 0)
    lane_id = lax.broadcasted_iota(jnp.int32, (8, LANES), 1)
    pick = ((row_id == 0) & (lane_id == LANES - 1)) | ((row_id == 1) & (lane_id == 0))
    return jnp.where(pick, 1.0, 0.0).astype(bf16)


def pack_kernel(dims, pieces, grid_hbm, out_ref, msg, held, sems):
    width, devices, planes = dims
    depth = devices * planes
    count = sum(n for _, n in pieces)
    rows = COMPS * count
    used = planes * rows
    total = out_ref.shape[1]
    copies = []
    for c in range(COMPS):
        off = c * count
        for x, n in pieces:
            copy = pltpu.make_async_copy(
                grid_hbm.at[pl.ds((c * width + x) * depth, n * depth), :],
                held.at[pl.ds(off * depth, n * depth), :],
                sems.at[len(copies)],
            )
            copy.start()
            copies.append(copy)
            off += n
    pick = side_picker()
    for j in range(devices):
        msg[pl.ds(j * total + used, total - used), :] = jnp.zeros((total - used, LANES), f32)
    for c in range(COMPS):
        for i in range(len(pieces)):
            copies[c * len(pieces) + i].wait()
        for j in range(devices):
            for p in range(planes):
                msg[pl.ds(j * total + p * rows + c * count, count), :] = held[
                    pl.ds(c * count * depth + j * planes + p, count, stride=depth), :
                ]
    for j in range(devices):
        for p in range(planes):
            block = msg[pl.ds(j * total + p * rows, rows), :].astype(bf16)
            edge = lax.dot_general(pick, block, NT, preferred_element_type=f32)
            right = (j + 1) % devices
            left = (j - 1) % devices
            msg[pl.ds(right * total + used + 2 * p, 1), 0:rows] = edge[0:1]
            msg[pl.ds(left * total + used + 2 * p + 1, 1), 0:rows] = edge[1:2]
    for j in range(devices):
        out_ref[j] = msg[pl.ds(j * total, total), :].astype(bf16)


def edge_kernel(planes, count, recv_ref, low_ref, high_ref, msg, out):
    devices = recv_ref.shape[0]
    used = planes * COMPS * count
    lines = planes * COMPS
    for s in range(devices):
        msg[...] = recv_ref[s].astype(f32)
        for e in range(lines):
            for side in range(2):
                at = e * count + side * (count - 1)
                out[side, pl.ds(s * lines + e, 1), :] = msg[pl.ds(at, 1), :]
        for side in range(2):
            out[side, pl.ds(devices * lines + s * 2 * planes, 2 * planes), :] = msg[pl.ds(used, 2 * planes), :]
    low_ref[...] = out[0].astype(bf16)
    high_ref[...] = out[1].astype(bf16)


def lane_of_x(local, c, count, ghosts):
    if not ghosts:
        return c * count + local
    lane = c * count + local - 1
    lane = jnp.where(local == 0, LANES // 2 + c * count + count - 1, lane)
    return jnp.where(local == count + 1, LANES // 2 + c * count, lane)


def same_cell(c, count, ghosts, depth, rows):
    local = lax.broadcasted_iota(jnp.int32, (rows, LANES), 0) // depth
    col = lax.broadcasted_iota(jnp.int32, (rows, LANES), 1)
    return jnp.where(col == lane_of_x(local, c, count, ghosts), 1.0, 0.0).astype(bf16)


def side_lane(depth, shape, dim):
    ghost = lax.broadcasted_iota(jnp.int32, shape, dim)
    lane = lax.broadcasted_iota(jnp.int32, shape, 1 - dim)
    hit = ((ghost < depth) & (lane == LANES - 1)) | ((ghost >= depth) & (lane == 0))
    return jnp.where(hit, 1.0, 0.0).astype(bf16)


def particle_kernel(dims, plan, *refs):
    width, devices, planes, subs_x, subs_y, slots, chunk = dims
    count, moves, ghosts, starts, strips, writes_all = plan
    counts_ref, recv_ref, vel_ref, frac_ref, tau_ref, cells_ref = refs[:6]
    refs = refs[6:]
    if ghosts:
        before_ref, after_ref = refs[:2]
        refs = refs[2:]
    if writes_all:
        other_ref = refs[0]
        refs = refs[1:]
    vel_out_ref, send_ref, msg, rows_buf, ghost, field, deposit, prep, ints = refs
    held = count + 2 if ghosts else count
    depth = devices * planes
    tile_x = width // subs_x
    tile_y = LANES // subs_y
    total = recv_ref.shape[1]
    rows = COMPS * count
    used = planes * rows
    cells = held * depth
    near = 4
    pair = 2 * depth
    pairs = tile_x // 2
    strip_rows = tile_x * depth
    core = len(starts) * strip_rows
    block = near * depth

    if writes_all:
        others = [a for a in range(subs_x) if a not in strips]
        for c in range(COMPS):
            for i, a in enumerate(others):
                vel_out_ref[c, a] = other_ref[c, i]

    lines = planes * COMPS
    for s in range(devices):
        msg[pl.ds(0, total), :] = recv_ref[s].astype(f32)
        for p in range(planes):
            z = s * planes + p
            for c in range(COMPS):
                for off, n, local in moves:
                    rows_buf[pl.ds(c * cells + local * depth + z, n, stride=depth), :] = msg[
                        pl.ds(p * rows + c * count + off, n), :
                    ]
            ghost[pl.ds(z, 1), :] = msg[pl.ds(used + 2 * p, 1), :]
            ghost[pl.ds(depth + z, 1), :] = msg[pl.ds(used + 2 * p + 1, 1), :]
    if ghosts:
        lane8 = lax.broadcasted_iota(jnp.int32, (2 * depth, LANES), 1)
        for side, ref in enumerate((before_ref, after_ref)):
            msg[pl.ds(0, ref.shape[0]), :] = ref[...].astype(f32)
            for s in range(devices):
                for p in range(planes):
                    z = s * planes + p
                    for c in range(COMPS):
                        at = c * cells + side * (held - 1) * depth + z
                        rows_buf[pl.ds(at, 1), :] = msg[pl.ds(s * lines + p * COMPS + c, 1), :]
            turned = []
            for lr in range(2):
                turned.append(msg[pl.ds(devices * lines + lr, depth, stride=2), :])
            turned = jnp.roll(jnp.concatenate(turned, axis=0), LANES // 2, axis=1)
            wanted = (lane8 - LANES // 2) % count == (count - 1 if side == 0 else 0)
            ghost[...] = jnp.where((lane8 >= LANES // 2) & wanted, turned, ghost[...])
    own_z = lax.broadcasted_iota(jnp.int32, (cells, 2 * depth), 0) % depth
    own_z = own_z == lax.broadcasted_iota(jnp.int32, (cells, 2 * depth), 1) % depth
    lane = lax.broadcasted_iota(jnp.int32, (cells, LANES), 1)
    strip_lane = lane[:strip_rows]
    for c in range(COMPS):
        at = pl.ds(c * cells, cells)
        wide = lax.dot_general(
            same_cell(c, count, ghosts, depth, cells), ghost[...].astype(bf16), NT, preferred_element_type=f32
        )
        wide = jnp.where(own_z, wide, 0.0).astype(bf16)
        outer = jnp.dot(wide, side_lane(depth, (2 * depth, LANES), 0), preferred_element_type=f32)
        inner = rows_buf[at, :]
        lower = jnp.where(lane == LANES - 1, outer, inner)
        upper = jnp.where(lane == 0, outer, inner)
        for side, value in enumerate((lower, upper)):
            moved = jnp.roll(value, LANES // 2, axis=1)
            for b in range(side * subs_y // 2, (side + 1) * subs_y // 2):
                first_half = (strip_lane - (b * tile_y - 16)) % LANES < LANES // 2
                for k, start in enumerate(starts):
                    r = start * depth
                    field[b, pl.ds(c * core + k * strip_rows, strip_rows), :] = jnp.where(
                        first_half, value[r : r + strip_rows], moved[r + pair : r + pair + strip_rows]
                    ).astype(bf16)

    x_rows = lax.broadcasted_iota(jnp.int32, (8, chunk), 0)
    z_rows = lax.broadcasted_iota(jnp.int32, (depth, chunk), 0)
    y_rows = lax.broadcasted_iota(jnp.int32, (tile_y + 16, chunk), 0) - 8

    def strip(k, carry):
        a = strips[0] + k * (strips[1] - strips[0])
        place_a = k if not writes_all else a
        for d in range(COMPS):
            f = frac_ref[d, a]
            prep[3 * d] = 0.5 * (0.5 - f) ** 2
            prep[3 * d + 1] = 0.75 - f * f
            prep[3 * d + 2] = 0.5 * (0.5 + f) ** 2
        prep[9] = step_dt / tau_ref[a]
        cell = cells_ref[a]
        ints[0] = cell // (tile_y * depth)
        ints[1] = cell // depth % tile_y
        ints[2] = cell % depth
        first = k * strip_rows

        for b in range(subs_y):
            filled = counts_ref[a, b]
            blocks = tile_x * depth // block
            data = jnp.concatenate(
                [
                    jnp.concatenate(
                        [
                            field[b, pl.ds(pl.multiple_of(c * core + first + t * block, block), block), :]
                            for t in range(blocks)
                        ],
                        axis=1,
                    )
                    for c in range(COMPS)
                ],
                axis=0,
            )
            acc = None
            for start in range(0, slots, chunk):
                at = slice(start, start + chunk)
                row = lambda i: prep[i, b : b + 1, at]
                xc, yc, zc = (ints[i, b : b + 1, at] for i in range(3))
                here = lax.broadcasted_iota(jnp.int32, (1, chunk), 1) + start < filled
                dx = x_rows - (xc & 1)
                wx = jnp.where(
                    dx == 0, row(0), jnp.where(dx == 1, row(1), jnp.where(dx == 2, row(2), 0.0))
                )
                dy = y_rows - yc
                y_low, y_mid, y_high = (jnp.where(here, row(3 + i), 0.0) for i in range(3))
                wy = jnp.where(
                    dy == -1, y_low, jnp.where(dy == 0, y_mid, jnp.where(dy == 1, y_high, 0.0))
                )
                dz = (z_rows - zc + 1) & (depth - 1)
                wz = jnp.where(
                    dz == 0, row(6), jnp.where(dz == 1, row(7), jnp.where(dz == 2, row(8), 0.0))
                )
                groups = LANES // 8
                half_groups = groups // 2
                blank = jnp.zeros((8, chunk), f32)
                pieces = [blank] * (groups * blocks)
                for q in range(pairs):
                    chosen = xc >> 1 == q
                    for g in range(tile_y // 8 + 2):
                        place = (b * tile_y // 8 - 1 + g + (q % 2) * half_groups) % groups
                        pieces[q // 2 * groups + place] = jnp.where(chosen, wy[8 * g : 8 * g + 8], 0.0)
                wy = jnp.concatenate(pieces, axis=0).astype(bf16)
                raw = jnp.dot(data, wy, preferred_element_type=f32)
                rate = row(9)
                shares = []
                for c in range(COMPS):
                    found = None
                    for i in range(near):
                        part = None
                        for g in range(depth // 8):
                            at8 = c * block + i * depth + 8 * g
                            term = raw[at8 : at8 + 8] * wz[8 * g : 8 * g + 8]
                            part = term if part is None else part + term
                        part = part * wx[i : i + 1]
                        found = part if found is None else found + part
                    interp = jnp.sum(found, axis=0, keepdims=True)
                    velocity = vel_ref[c, a, b : b + 1, at]
                    change = rate * (interp - velocity)
                    vel_out_ref[c, place_a, b : b + 1, at] = jnp.where(here, velocity + change, velocity)
                    pull = jnp.where(here, -mass_load * change, 0.0) * wx
                    shares = shares + [(pull[i : i + 1] * wz).astype(bf16) for i in range(near)]
                part = lax.dot_general(
                    jnp.concatenate(shares, axis=0), wy, NT, preferred_element_type=f32
                )
                acc = part if acc is None else acc + part
            for c in range(COMPS):
                for t in range(blocks):
                    base = pl.multiple_of(c * core + first + t * block, block)
                    deposit[b, pl.ds(base, block), :] = acc[
                        c * block : (c + 1) * block, t * LANES : (t + 1) * LANES
                    ]
        return carry

    lax.fori_loop(0, len(strips), strip, 0)

    gathered = jnp.zeros((2 * depth, LANES), f32)
    empty = jnp.zeros((pair, LANES), f32)
    for c in range(COMPS):
        at = pl.ds(c * cells, cells)
        sides = []
        for side in range(2):
            found = []
            for k in range(len(starts)):
                even = odd = None
                for b in range(side * subs_y // 2, (side + 1) * subs_y // 2):
                    value = deposit[b, pl.ds(c * core + k * strip_rows, strip_rows), :]
                    first_half = (strip_lane - (b * tile_y - 16)) % LANES < LANES // 2
                    one = jnp.where(first_half, value, 0.0)
                    two = jnp.where(first_half, 0.0, value)
                    even = one if even is None else even + one
                    odd = two if odd is None else odd + two
                moved = jnp.roll(odd, LANES // 2, axis=1)
                found.append(
                    jnp.concatenate([even, empty], axis=0) + jnp.concatenate([empty, moved], axis=0)
                )
            shared = strip_rows + pair - (starts[1] - starts[0]) * depth
            if shared == 0:
                sides.append(jnp.concatenate(found, axis=0))
            else:
                keep = strip_rows + pair - shared
                middle = found[0][keep:] + found[1][:shared]
                sides.append(jnp.concatenate([found[0][:keep], middle, found[1][shared:]], axis=0))
        lower, upper = sides
        first_lane = lane == 0
        last_lane = lane == LANES - 1
        rows_buf[at, :] = jnp.where(last_lane, 0.0, lower) + jnp.where(first_lane, 0.0, upper)
        outer = jnp.where(last_lane, lower, jnp.where(first_lane, upper, 0.0)).astype(bf16)
        wide = jnp.dot(outer, side_lane(depth, (LANES, 2 * depth), 1), preferred_element_type=f32)
        wide = jnp.where(own_z, wide, 0.0).astype(bf16)
        gathered = gathered + lax.dot_general(
            wide, same_cell(c, held, False, depth, cells), (((0,), (0,)), ((), ())), preferred_element_type=f32
        )
    ghost[...] = gathered
    rows = COMPS * held
    used = planes * rows
    total = send_ref.shape[1]
    for s in range(devices):
        if total > used + 2 * planes:
            msg[pl.ds(used, total - used), :] = jnp.zeros((total - used, LANES), f32)
        for p in range(planes):
            z = s * planes + p
            for c in range(COMPS):
                msg[pl.ds(p * rows + c * held, held), :] = rows_buf[
                    pl.ds(c * cells + z, held, stride=depth), :
                ]
            msg[pl.ds(used + 2 * p, 1), :] = ghost[pl.ds(z, 1), :]
            msg[pl.ds(used + 2 * p + 1, 1), :] = ghost[pl.ds(depth + z, 1), :]
        send_ref[s] = msg[pl.ds(0, total), :].astype(bf16)


def particle_call(dims, plan, counts, recv, part_vel, part_frac, stokes_time, cells, extra):
    width, devices, planes, subs_x, subs_y, slots, chunk = dims
    count, moves, ghosts, starts, strips, writes_all = plan
    vmem = pl.BlockSpec(memory_space=pltpu.VMEM)
    held = count + 2 if ghosts else count
    depth = devices * planes
    total_out = message_rows(planes, held)
    core_rows = COMPS * len(strips) * (width // subs_x) * depth
    vel_shape = part_vel.shape if writes_all else (COMPS, len(strips), subs_y, slots)
    return pl.pallas_call(
        functools.partial(particle_kernel, dims, plan),
        out_shape=(
            jax.ShapeDtypeStruct(vel_shape, f32),
            jax.ShapeDtypeStruct((devices, total_out, LANES), bf16),
        ),
        in_specs=[pl.BlockSpec(memory_space=pltpu.SMEM)] + [vmem] * (5 + len(extra)),
        out_specs=(vmem, vmem),
        scratch_shapes=[
            pltpu.VMEM((devices * planes * 5, LANES), f32),
            pltpu.VMEM((COMPS * held * depth + 8 * depth, LANES), f32),
            pltpu.VMEM((2 * depth, LANES), f32),
            pltpu.VMEM((subs_y, core_rows, LANES), bf16),
            pltpu.VMEM((subs_y, core_rows, LANES), f32),
            pltpu.VMEM((10, subs_y, slots), f32),
            pltpu.VMEM((3, subs_y, slots), jnp.int32),
        ],
        compiler_params=pltpu.CompilerParams(vmem_limit_bytes=VMEM_LIMIT),
        cost_estimate=pl.CostEstimate(flops=int(8e9), bytes_accessed=int(2e7), transcendentals=0),
        name="particles_outer" if ghosts else "particles_inner",
    )(counts, recv, part_vel, part_frac, stokes_time, cells, *extra)


def gather_kernel(planes, held, skip, recv_ref, out_ref, *refs):
    msg = refs[-1]
    rows = COMPS * held
    used = planes * rows
    count = recv_ref.shape[0]
    inner = held - 2 * skip
    for j in range(count):
        msg[j] = recv_ref[j].astype(f32)
    place = side_picker()
    for j in range(count):
        left = (j - 1) % count
        right = (j + 1) % count
        lanes = slice(j * LANES, (j + 1) * LANES)
        lows, highs = [], []
        for p in range(planes):
            pair = jnp.concatenate(
                [
                    msg[right, used + 2 * p : used + 2 * p + 1, :],
                    msg[left, used + 2 * p + 1 : used + 2 * p + 2, :],
                    jnp.zeros((6, LANES), f32),
                ],
                axis=0,
            ).astype(bf16)
            added = lax.dot_general(
                pair, place, (((0,), (0,)), ((), ())), preferred_element_type=f32
            )
            block = msg[j, p * rows : (p + 1) * rows, :] + added[:rows]
            for c in range(COMPS):
                e = p * COMPS + c
                at = c * held
                lows.append(block[at : at + 1])
                highs.append(block[at + held - 1 : at + held])
                out_ref[pl.ds(e * inner, inner), lanes] = block[at + skip : at + skip + inner]
        if skip:
            refs[0][:, lanes] = jnp.concatenate(lows, axis=0).astype(bf16)
            refs[1][:, lanes] = jnp.concatenate(highs, axis=0).astype(bf16)


def gather_call(planes, held, skip, recv):
    devices = recv.shape[0]
    length = devices * LANES
    vmem = pl.BlockSpec(memory_space=pltpu.VMEM)
    lines = planes * COMPS
    shapes = [jax.ShapeDtypeStruct((lines * (held - 2 * skip), length), f32)]
    if skip:
        shapes += [jax.ShapeDtypeStruct((lines, length), bf16)] * 2
    return pl.pallas_call(
        functools.partial(gather_kernel, planes, held, skip),
        out_shape=tuple(shapes),
        in_specs=[vmem],
        out_specs=(vmem,) * len(shapes),
        scratch_shapes=[pltpu.VMEM(recv.shape, f32)],
        compiler_params=pltpu.CompilerParams(vmem_limit_bytes=VMEM_LIMIT),
        cost_estimate=pl.CostEstimate(flops=int(1e8), bytes_accessed=int(2e6), transcendentals=0),
        name="gather",
    )(recv)


def filter_kernel(
    dims, outer_pieces, inner_piece, grid_ref, outer_ref, inner_ref, from_low_ref, from_high_ref,
    high_ref, low_ref, out_ref, mixed, dep,
):
    width, devices, planes = dims
    depth = devices * planes
    outer_count = sum(n for _, n in outer_pieces)
    inner_x, inner_count = inner_piece
    for p in range(planes):
        for c in range(COMPS):
            e = p * COMPS + c
            dep[...] = jnp.zeros(dep.shape, f32)
            off = e * outer_count
            for x, n in outer_pieces:
                dep[pl.ds(x, n), :] = outer_ref[pl.ds(off, n), :]
                off += n
            dep[pl.ds(inner_x, inner_count), :] += inner_ref[pl.ds(e * inner_count, inner_count), :]
            dep[pl.ds(0, 1), :] += from_low_ref[e : e + 1, :].astype(f32)
            dep[pl.ds(width - 1, 1), :] += from_high_ref[e : e + 1, :].astype(f32)
            for j in range(devices):
                lanes = slice(j * LANES, (j + 1) * LANES)
                fluid = grid_ref[pl.ds(c * width * depth + j * planes + p, width, stride=depth), :]
                mixed[pl.ds(e * width, width), lanes] = fluid + dep[0:width, lanes].astype(bf16).astype(f32)
    folds = high_ref.shape[1]
    block = high_ref.shape[2]
    sides = []
    for sign in range(2):
        highs, lows = [], []
        for i in range(folds):
            one = mixed[:, i * block : (i + 1) * block]
            two = mixed[:, (i + folds) * block : (i + folds + 1) * block]
            value = one + two if sign == 0 else one - two
            high = value.astype(bf16)
            highs.append(high)
            lows.append((value - high.astype(f32)).astype(bf16))
        sides.append((highs, lows))
    for o in range(folds):
        results = []
        for sign in range(2):
            highs, lows = sides[sign]
            sums = {1: None, -1: None}
            for i in range(folds):
                d = (o - i) % folds
                key = -1 if sign == 1 and o < i else 1
                part = jnp.dot(highs[i], high_ref[sign, d], preferred_element_type=f32)
                part = part + jnp.dot(lows[i], high_ref[sign, d], preferred_element_type=f32)
                part = part + jnp.dot(highs[i], low_ref[sign, d], preferred_element_type=f32)
                sums[key] = part if sums[key] is None else sums[key] + part
            results.append(sums[1] if sums[-1] is None else sums[1] - sums[-1])
        for flip in range(2):
            value = results[0] + results[1] if flip == 0 else results[0] - results[1]
            for half in range(block // LANES):
                j = (o + flip * folds) * (block // LANES) + half
                for p in range(planes):
                    for c in range(COMPS):
                        e = p * COMPS + c
                        out_ref[pl.ds(c * width * depth + j * planes + p, width, stride=depth), :] = value[
                            e * width : (e + 1) * width, half * LANES : (half + 1) * LANES
                        ]


def message_rows(planes, held):
    return -(-(planes * COMPS * held + 2 * planes) // 16) * 16


def exchange(low, high):
    size = lax.axis_size("px")
    even = lax.axis_index("px") % 2 == 0
    first = [(i, i ^ 1) for i in range(size)]
    second = [(i, (i + 1) % size if i % 2 else (i - 1) % size) for i in range(size)]
    far = lax.ppermute(jnp.where(even, low, high), "px", second)
    close = lax.ppermute(jnp.where(even, high, low), "px", first)
    return jnp.where(even, far, close), jnp.where(even, close, far)


def per_device(fluid, part_vel, part_frac, stokes_time, cells, counts):
    devices = lax.axis_size("py")
    _, width, planes, length = fluid.shape
    subs_x, subs_y, slots = stokes_time.shape
    depth = planes * devices
    tile_x = width // subs_x
    params = pltpu.CompilerParams(vmem_limit_bytes=VMEM_LIMIT)
    vmem = pl.BlockSpec(memory_space=pltpu.VMEM)
    dims = (width, devices, planes)

    outer = ((0, tile_x + 1), (width - tile_x - 1, tile_x + 1))
    inner = (tile_x - 1, width - 2 * tile_x + 2)
    outer_count = 2 * (tile_x + 1)
    inner_count = inner[1]
    grid = fluid.reshape(COMPS * width, planes, devices, LANES).transpose(0, 2, 1, 3)
    grid = grid.reshape(COMPS * width * depth, LANES)
    outer_rows = message_rows(planes, outer_count)
    inner_rows = message_rows(planes, inner_count)
    hbm = pl.BlockSpec(memory_space=pltpu.HBM)

    def pack(pieces, total, limit):
        count = sum(n for _, n in pieces)
        return pl.pallas_call(
            functools.partial(pack_kernel, dims, pieces),
            out_shape=jax.ShapeDtypeStruct((devices, total, LANES), bf16),
            in_specs=[hbm],
            out_specs=vmem,
            scratch_shapes=[
                pltpu.VMEM((devices * total, LANES), f32),
                pltpu.VMEM((COMPS * count * depth + 8 * depth, LANES), f32),
                pltpu.SemaphoreType.DMA((COMPS * len(pieces),)),
            ],
            compiler_params=pltpu.CompilerParams(vmem_limit_bytes=limit),
            cost_estimate=pl.CostEstimate(flops=int(1e8), bytes_accessed=int(2e6), transcendentals=0),
            name="pack",
        )(grid)

    send_outer = pack(outer, outer_rows, VMEM_MOST)
    send_inner = pack((inner,), inner_rows, VMEM_MOST)
    recv_outer = lax.all_to_all(send_outer, "py", 0, 0, tiled=True)
    recv_outer, send_inner = lax.optimization_barrier((recv_outer, send_inner))
    recv_inner = lax.all_to_all(send_inner, "py", 0, 0, tiled=True)

    edge_rows = devices * planes * (COMPS + 2)
    low, high = pl.pallas_call(
        functools.partial(edge_kernel, planes, outer_count),
        out_shape=(jax.ShapeDtypeStruct((edge_rows, LANES), bf16),) * 2,
        in_specs=[vmem],
        out_specs=(vmem, vmem),
        scratch_shapes=[pltpu.VMEM((outer_rows, LANES), f32), pltpu.VMEM((2, edge_rows, LANES), f32)],
        compiler_params=params,
        name="edges",
    )(recv_outer)
    before, after = exchange(low, high)

    sizes = (width, devices, planes, subs_x, subs_y, slots, min(256, slots))
    half = tile_x + 1
    outer_plan = (
        outer_count, ((0, half, 1), (half, half, half + 1)), True, (0, tile_x + 2), (0, subs_x - 1), False,
    )
    inner_plan = (inner_count, ((0, inner_count, 0),), False, (0, tile_x), (1, 2), True)
    vel_outer, back_outer = particle_call(
        sizes, outer_plan, counts, recv_outer, part_vel, part_frac, stokes_time, cells, (before, after)
    )
    pencil_outer = lax.all_to_all(back_outer, "py", 0, 0, tiled=True)
    vel_next, back_inner = particle_call(
        sizes, inner_plan, counts, recv_inner, part_vel, part_frac, stokes_time, cells, (vel_outer,)
    )
    pencil_outer, back_inner = lax.optimization_barrier((pencil_outer, back_inner))
    pencil_inner = lax.all_to_all(back_inner, "py", 0, 0, tiled=True)
    dep_outer, low, high = gather_call(planes, outer_count + 2, 1, pencil_outer)
    from_low, from_high = exchange(low, high)
    (dep_inner,) = gather_call(planes, inner_count, 0, pencil_inner)
    taps_high, taps_low = filter_blocks(length, 256)
    out = pl.pallas_call(
        functools.partial(filter_kernel, dims, outer, inner),
        out_shape=jax.ShapeDtypeStruct(grid.shape, f32),
        in_specs=[vmem] * 7,
        out_specs=vmem,
        scratch_shapes=[
            pltpu.VMEM((planes * COMPS * width, length), f32),
            pltpu.VMEM((width + 8, length), f32),
        ],
        compiler_params=params,
        name="filter",
    )(grid, dep_outer, dep_inner, from_low, from_high, jnp.asarray(taps_high), jnp.asarray(taps_low))
    out = out.reshape(COMPS * width, devices, planes, LANES).transpose(0, 2, 1, 3)
    return out.reshape(fluid.shape), vel_next


def solution(mesh):
    placed = (
        P(None, "px", "py", None),
        P(None, "px", "py", None),
        P(None, "px", "py", None),
        P("px", "py", None),
        P("px", "py", None),
        P("px", "py"),
    )
    return jax.shard_map(
        per_device,
        mesh=mesh,
        in_specs=placed,
        out_specs=(P(None, "px", "py", None), P(None, "px", "py", None)),
        check_vma=False,
    )
```

```python
import functools
import math

import jax
import jax.numpy as jnp
import numpy as np
from jax import lax
from jax.experimental import pallas as pl
from jax.experimental.pallas import tpu as pltpu
from jax.sharding import PartitionSpec as P

mass_load = 4.0
step_dt = 0.5
viscous_step = 0.25
forcing_gain = 1.5
forced_modes = 4

COMPS = 3
LANES = 128
VMEM_LIMIT = 24 * 1024 * 1024
VMEM_MOST = 58 * 1024 * 1024
f32 = jnp.float32
bf16 = jnp.bfloat16
NT = (((1,), (1,)), ((), ()))


def filter_blocks(length, width):
    k = np.fft.fftfreq(length, 1.0 / length)
    angle = 2.0 * math.pi * k / length
    gain = np.exp(-viscous_step * angle * angle)
    gain = gain * np.where((abs(k) >= 1) & (abs(k) <= forced_modes), 1.0 + forcing_gain, 1.0)
    taps = np.fft.ifft(gain).real
    blocks = length // width
    half = blocks // 2
    inner = np.arange(width)
    full = []
    for d in range(blocks):
        full.append(taps[(width * d + inner[None, :] - inner[:, None]) % length])
    sums = np.stack([0.5 * (full[d] + full[d + half]) for d in range(half)])
    diffs = np.stack([0.5 * (full[d] - full[d + half]) for d in range(half)])
    both = np.stack([sums, diffs]).astype(np.float32)
    high = both.astype(jnp.bfloat16)
    low = (both - high.astype(np.float32)).astype(jnp.bfloat16)
    return high, low


def side_picker():
    row_id = lax.broadcasted_iota(jnp.int32, (8, LANES), 0)
    lane_id = lax.broadcasted_iota(jnp.int32, (8, LANES), 1)
    pick = ((row_id == 0) & (lane_id == LANES - 1)) | ((row_id == 1) & (lane_id == 0))
    return jnp.where(pick, 1.0, 0.0).astype(bf16)


def pack_kernel(dims, pieces, grid_hbm, out_ref, msg, held, sems):
    width, devices, planes = dims
    depth = devices * planes
    count = sum(n for _, n in pieces)
    rows = COMPS * count
    used = planes * rows
    total = out_ref.shape[1]
    copies = []
    for c in range(COMPS):
        off = c * count
        for x, n in pieces:
            copy = pltpu.make_async_copy(
                grid_hbm.at[pl.ds((c * width + x) * depth, n * depth), :],
                held.at[pl.ds(off * depth, n * depth), :],
                sems.at[len(copies)],
            )
            copy.start()
            copies.append(copy)
            off += n
    pick = side_picker()
    for j in range(devices):
        msg[pl.ds(j * total + used, total - used), :] = jnp.zeros((total - used, LANES), f32)
    for c in range(COMPS):
        for i in range(len(pieces)):
            copies[c * len(pieces) + i].wait()
        for j in range(devices):
            for p in range(planes):
                msg[pl.ds(j * total + p * rows + c * count, count), :] = held[
                    pl.ds(c * count * depth + j * planes + p, count, stride=depth), :
                ]
    for j in range(devices):
        for p in range(planes):
            block = msg[pl.ds(j * total + p * rows, rows), :].astype(bf16)
            edge = lax.dot_general(pick, block, NT, preferred_element_type=f32)
            right = (j + 1) % devices
            left = (j - 1) % devices
            msg[pl.ds(right * total + used + 2 * p, 1), 0:rows] = edge[0:1]
            msg[pl.ds(left * total + used + 2 * p + 1, 1), 0:rows] = edge[1:2]
    for j in range(devices):
        out_ref[j] = msg[pl.ds(j * total, total), :].astype(bf16)


def edge_kernel(planes, count, recv_ref, low_ref, high_ref, msg, out):
    devices = recv_ref.shape[0]
    used = planes * COMPS * count
    lines = planes * COMPS
    for s in range(devices):
        msg[...] = recv_ref[s].astype(f32)
        for e in range(lines):
            for side in range(2):
                at = e * count + side * (count - 1)
                out[side, pl.ds(s * lines + e, 1), :] = msg[pl.ds(at, 1), :]
        for side in range(2):
            out[side, pl.ds(devices * lines + s * 2 * planes, 2 * planes), :] = msg[pl.ds(used, 2 * planes), :]
    low_ref[...] = out[0].astype(bf16)
    high_ref[...] = out[1].astype(bf16)


def lane_of_x(local, c, count, ghosts):
    if not ghosts:
        return c * count + local
    lane = c * count + local - 1
    lane = jnp.where(local == 0, LANES // 2 + c * count + count - 1, lane)
    return jnp.where(local == count + 1, LANES // 2 + c * count, lane)


def same_cell(c, count, ghosts, depth, rows):
    local = lax.broadcasted_iota(jnp.int32, (rows, LANES), 0) // depth
    col = lax.broadcasted_iota(jnp.int32, (rows, LANES), 1)
    return jnp.where(col == lane_of_x(local, c, count, ghosts), 1.0, 0.0).astype(bf16)


def side_lane(depth, shape, dim):
    ghost = lax.broadcasted_iota(jnp.int32, shape, dim)
    lane = lax.broadcasted_iota(jnp.int32, shape, 1 - dim)
    hit = ((ghost < depth) & (lane == LANES - 1)) | ((ghost >= depth) & (lane == 0))
    return jnp.where(hit, 1.0, 0.0).astype(bf16)


def particle_kernel(dims, plan, *refs):
    width, devices, planes, subs_x, subs_y, slots, chunk = dims
    count, moves, ghosts, starts, strips, writes_all = plan
    counts_ref, recv_ref, vel_ref, frac_ref, tau_ref, cells_ref = refs[:6]
    refs = refs[6:]
    if ghosts:
        before_ref, after_ref = refs[:2]
        refs = refs[2:]
    if writes_all:
        other_ref = refs[0]
        refs = refs[1:]
    vel_out_ref, send_ref, msg, rows_buf, ghost, field, deposit, prep, ints = refs
    held = count + 2 if ghosts else count
    depth = devices * planes
    tile_x = width // subs_x
    tile_y = LANES // subs_y
    total = recv_ref.shape[1]
    rows = COMPS * count
    used = planes * rows
    cells = held * depth
    near = 4
    pair = 2 * depth
    pairs = tile_x // 2
    strip_rows = tile_x * depth
    core = len(starts) * strip_rows
    block = near * depth

    if writes_all:
        others = [a for a in range(subs_x) if a not in strips]
        for c in range(COMPS):
            for i, a in enumerate(others):
                vel_out_ref[c, a] = other_ref[c, i]

    lines = planes * COMPS
    for s in range(devices):
        msg[pl.ds(0, total), :] = recv_ref[s].astype(f32)
        for p in range(planes):
            z = s * planes + p
            for c in range(COMPS):
                for off, n, local in moves:
                    rows_buf[pl.ds(c * cells + local * depth + z, n, stride=depth), :] = msg[
                        pl.ds(p * rows + c * count + off, n), :
                    ]
            ghost[pl.ds(z, 1), :] = msg[pl.ds(used + 2 * p, 1), :]
            ghost[pl.ds(depth + z, 1), :] = msg[pl.ds(used + 2 * p + 1, 1), :]
    if ghosts:
        lane8 = lax.broadcasted_iota(jnp.int32, (2 * depth, LANES), 1)
        for side, ref in enumerate((before_ref, after_ref)):
            msg[pl.ds(0, ref.shape[0]), :] = ref[...].astype(f32)
            for s in range(devices):
                for p in range(planes):
                    z = s * planes + p
                    for c in range(COMPS):
                        at = c * cells + side * (held - 1) * depth + z
                        rows_buf[pl.ds(at, 1), :] = msg[pl.ds(s * lines + p * COMPS + c, 1), :]
            turned = []
            for lr in range(2):
                turned.append(msg[pl.ds(devices * lines + lr, depth, stride=2), :])
            turned = jnp.roll(jnp.concatenate(turned, axis=0), LANES // 2, axis=1)
            wanted = (lane8 - LANES // 2) % count == (count - 1 if side == 0 else 0)
            ghost[...] = jnp.where((lane8 >= LANES // 2) & wanted, turned, ghost[...])
    own_z = lax.broadcasted_iota(jnp.int32, (cells, 2 * depth), 0) % depth
    own_z = own_z == lax.broadcasted_iota(jnp.int32, (cells, 2 * depth), 1) % depth
    lane = lax.broadcasted_iota(jnp.int32, (cells, LANES), 1)
    strip_lane = lane[:strip_rows]
    for c in range(COMPS):
        at = pl.ds(c * cells, cells)
        wide = lax.dot_general(
            same_cell(c, count, ghosts, depth, cells), ghost[...].astype(bf16), NT, preferred_element_type=f32
        )
        wide = jnp.where(own_z, wide, 0.0).astype(bf16)
        outer = jnp.dot(wide, side_lane(depth, (2 * depth, LANES), 0), preferred_element_type=f32)
        inner = rows_buf[at, :]
        lower = jnp.where(lane == LANES - 1, outer, inner)
        upper = jnp.where(lane == 0, outer, inner)
        for side, value in enumerate((lower, upper)):
            moved = jnp.roll(value, LANES // 2, axis=1)
            for b in range(side * subs_y // 2, (side + 1) * subs_y // 2):
                first_half = (strip_lane - (b * tile_y - 16)) % LANES < LANES // 2
                for k, start in enumerate(starts):
                    r = start * depth
                    field[b, pl.ds(c * core + k * strip_rows, strip_rows), :] = jnp.where(
                        first_half, value[r : r + strip_rows], moved[r + pair : r + pair + strip_rows]
                    ).astype(bf16)

    x_rows = lax.broadcasted_iota(jnp.int32, (8, chunk), 0)
    z_rows = lax.broadcasted_iota(jnp.int32, (depth, chunk), 0)
    y_rows = lax.broadcasted_iota(jnp.int32, (tile_y + 16, chunk), 0) - 8

    def strip(k, carry):
        a = strips[0] + k * (strips[1] - strips[0])
        place_a = k if not writes_all else a
        for d in range(COMPS):
            f = frac_ref[d, a]
            prep[3 * d] = 0.5 * (0.5 - f) ** 2
            prep[3 * d + 1] = 0.75 - f * f
            prep[3 * d + 2] = 0.5 * (0.5 + f) ** 2
        prep[9] = step_dt / tau_ref[a]
        cell = cells_ref[a]
        ints[0] = cell // (tile_y * depth)
        ints[1] = cell // depth % tile_y
        ints[2] = cell % depth
        first = k * strip_rows

        for b in range(subs_y):
            filled = counts_ref[a, b]
            blocks = tile_x * depth // block
            data = jnp.concatenate(
                [
                    jnp.concatenate(
                        [
                            field[b, pl.ds(pl.multiple_of(c * core + first + t * block, block), block), :]
                            for t in range(blocks)
                        ],
                        axis=1,
                    )
                    for c in range(COMPS)
                ],
                axis=0,
            )
            acc = None
            for start in range(0, slots, chunk):
                at = slice(start, start + chunk)
                row = lambda i: prep[i, b : b + 1, at]
                xc, yc, zc = (ints[i, b : b + 1, at] for i in range(3))
                here = lax.broadcasted_iota(jnp.int32, (1, chunk), 1) + start < filled
                dx = x_rows - (xc & 1)
                wx = jnp.where(
                    dx == 0, row(0), jnp.where(dx == 1, row(1), jnp.where(dx == 2, row(2), 0.0))
                )
                dy = y_rows - yc
                y_low, y_mid, y_high = (jnp.where(here, row(3 + i), 0.0) for i in range(3))
                wy = jnp.where(
                    dy == -1, y_low, jnp.where(dy == 0, y_mid, jnp.where(dy == 1, y_high, 0.0))
                )
                dz = (z_rows - zc + 1) & (depth - 1)
                wz = jnp.where(
                    dz == 0, row(6), jnp.where(dz == 1, row(7), jnp.where(dz == 2, row(8), 0.0))
                )
                groups = LANES // 8
                half_groups = groups // 2
                blank = jnp.zeros((8, chunk), f32)
                pieces = [blank] * (groups * blocks)
                for q in range(pairs):
                    chosen = xc >> 1 == q
                    for g in range(tile_y // 8 + 2):
                        place = (b * tile_y // 8 - 1 + g + (q % 2) * half_groups) % groups
                        pieces[q // 2 * groups + place] = jnp.where(chosen, wy[8 * g : 8 * g + 8], 0.0)
                wy = jnp.concatenate(pieces, axis=0).astype(bf16)
                raw = jnp.dot(data, wy, preferred_element_type=f32)
                rate = row(9)
                shares = []
                for c in range(COMPS):
                    found = None
                    for i in range(near):
                        part = None
                        for g in range(depth // 8):
                            at8 = c * block + i * depth + 8 * g
                            term = raw[at8 : at8 + 8] * wz[8 * g : 8 * g + 8]
                            part = term if part is None else part + term
                        part = part * wx[i : i + 1]
                        found = part if found is None else found + part
                    interp = jnp.sum(found, axis=0, keepdims=True)
                    velocity = vel_ref[c, a, b : b + 1, at]
                    change = rate * (interp - velocity)
                    vel_out_ref[c, place_a, b : b + 1, at] = jnp.where(here, velocity + change, velocity)
                    pull = jnp.where(here, -mass_load * change, 0.0) * wx
                    shares = shares + [(pull[i : i + 1] * wz).astype(bf16) for i in range(near)]
                part = lax.dot_general(
                    jnp.concatenate(shares, axis=0), wy, NT, preferred_element_type=f32
                )
                acc = part if acc is None else acc + part
            for c in range(COMPS):
                for t in range(blocks):
                    base = pl.multiple_of(c * core + first + t * block, block)
                    deposit[b, pl.ds(base, block), :] = acc[
                        c * block : (c + 1) * block, t * LANES : (t + 1) * LANES
                    ]
        return carry

    lax.fori_loop(0, len(strips), strip, 0)

    gathered = jnp.zeros((2 * depth, LANES), f32)
    empty = jnp.zeros((pair, LANES), f32)
    for c in range(COMPS):
        at = pl.ds(c * cells, cells)
        sides = []
        for side in range(2):
            found = []
            for k in range(len(starts)):
                even = odd = None
                for b in range(side * subs_y // 2, (side + 1) * subs_y // 2):
                    value = deposit[b, pl.ds(c * core + k * strip_rows, strip_rows), :]
                    first_half = (strip_lane - (b * tile_y - 16)) % LANES < LANES // 2
                    one = jnp.where(first_half, value, 0.0)
                    two = jnp.where(first_half, 0.0, value)
                    even = one if even is None else even + one
                    odd = two if odd is None else odd + two
                moved = jnp.roll(odd, LANES // 2, axis=1)
                found.append(
                    jnp.concatenate([even, empty], axis=0) + jnp.concatenate([empty, moved], axis=0)
                )
            shared = strip_rows + pair - (starts[1] - starts[0]) * depth
            if shared == 0:
                sides.append(jnp.concatenate(found, axis=0))
            else:
                keep = strip_rows + pair - shared
                middle = found[0][keep:] + found[1][:shared]
                sides.append(jnp.concatenate([found[0][:keep], middle, found[1][shared:]], axis=0))
        lower, upper = sides
        first_lane = lane == 0
        last_lane = lane == LANES - 1
        rows_buf[at, :] = jnp.where(last_lane, 0.0, lower) + jnp.where(first_lane, 0.0, upper)
        outer = jnp.where(last_lane, lower, jnp.where(first_lane, upper, 0.0)).astype(bf16)
        wide = jnp.dot(outer, side_lane(depth, (LANES, 2 * depth), 1), preferred_element_type=f32)
        wide = jnp.where(own_z, wide, 0.0).astype(bf16)
        gathered = gathered + lax.dot_general(
            wide, same_cell(c, held, False, depth, cells), (((0,), (0,)), ((), ())), preferred_element_type=f32
        )
    ghost[...] = gathered
    rows = COMPS * held
    used = planes * rows
    total = send_ref.shape[1]
    for s in range(devices):
        if total > used + 2 * planes:
            msg[pl.ds(used, total - used), :] = jnp.zeros((total - used, LANES), f32)
        for p in range(planes):
            z = s * planes + p
            for c in range(COMPS):
                msg[pl.ds(p * rows + c * held, held), :] = rows_buf[
                    pl.ds(c * cells + z, held, stride=depth), :
                ]
            msg[pl.ds(used + 2 * p, 1), :] = ghost[pl.ds(z, 1), :]
            msg[pl.ds(used + 2 * p + 1, 1), :] = ghost[pl.ds(depth + z, 1), :]
        send_ref[s] = msg[pl.ds(0, total), :].astype(bf16)


def particle_call(dims, plan, counts, recv, part_vel, part_frac, stokes_time, cells, extra):
    width, devices, planes, subs_x, subs_y, slots, chunk = dims
    count, moves, ghosts, starts, strips, writes_all = plan
    vmem = pl.BlockSpec(memory_space=pltpu.VMEM)
    held = count + 2 if ghosts else count
    depth = devices * planes
    total_out = message_rows(planes, held)
    core_rows = COMPS * len(strips) * (width // subs_x) * depth
    vel_shape = part_vel.shape if writes_all else (COMPS, len(strips), subs_y, slots)
    return pl.pallas_call(
        functools.partial(particle_kernel, dims, plan),
        out_shape=(
            jax.ShapeDtypeStruct(vel_shape, f32),
            jax.ShapeDtypeStruct((devices, total_out, LANES), bf16),
        ),
        in_specs=[pl.BlockSpec(memory_space=pltpu.SMEM)] + [vmem] * (5 + len(extra)),
        out_specs=(vmem, vmem),
        scratch_shapes=[
            pltpu.VMEM((devices * planes * 5, LANES), f32),
            pltpu.VMEM((COMPS * held * depth + 8 * depth, LANES), f32),
            pltpu.VMEM((2 * depth, LANES), f32),
            pltpu.VMEM((subs_y, core_rows, LANES), bf16),
            pltpu.VMEM((subs_y, core_rows, LANES), f32),
            pltpu.VMEM((10, subs_y, slots), f32),
            pltpu.VMEM((3, subs_y, slots), jnp.int32),
        ],
        compiler_params=pltpu.CompilerParams(vmem_limit_bytes=VMEM_LIMIT),
        cost_estimate=pl.CostEstimate(flops=int(8e9), bytes_accessed=int(2e7), transcendentals=0),
        name="particles_outer" if ghosts else "particles_inner",
    )(counts, recv, part_vel, part_frac, stokes_time, cells, *extra)


def gather_kernel(planes, held, skip, recv_ref, out_ref, *refs):
    msg = refs[-1]
    rows = COMPS * held
    used = planes * rows
    count = recv_ref.shape[0]
    inner = held - 2 * skip
    for j in range(count):
        msg[j] = recv_ref[j].astype(f32)
    place = side_picker()
    for j in range(count):
        left = (j - 1) % count
        right = (j + 1) % count
        lanes = slice(j * LANES, (j + 1) * LANES)
        lows, highs = [], []
        for p in range(planes):
            pair = jnp.concatenate(
                [
                    msg[right, used + 2 * p : used + 2 * p + 1, :],
                    msg[left, used + 2 * p + 1 : used + 2 * p + 2, :],
                    jnp.zeros((6, LANES), f32),
                ],
                axis=0,
            ).astype(bf16)
            added = lax.dot_general(
                pair, place, (((0,), (0,)), ((), ())), preferred_element_type=f32
            )
            block = msg[j, p * rows : (p + 1) * rows, :] + added[:rows]
            for c in range(COMPS):
                e = p * COMPS + c
                at = c * held
                lows.append(block[at : at + 1])
                highs.append(block[at + held - 1 : at + held])
                out_ref[pl.ds(e * inner, inner), lanes] = block[at + skip : at + skip + inner]
        if skip:
            refs[0][:, lanes] = jnp.concatenate(lows, axis=0).astype(bf16)
            refs[1][:, lanes] = jnp.concatenate(highs, axis=0).astype(bf16)


def gather_call(planes, held, skip, recv):
    devices = recv.shape[0]
    length = devices * LANES
    vmem = pl.BlockSpec(memory_space=pltpu.VMEM)
    lines = planes * COMPS
    shapes = [jax.ShapeDtypeStruct((lines * (held - 2 * skip), length), f32)]
    if skip:
        shapes += [jax.ShapeDtypeStruct((lines, length), bf16)] * 2
    return pl.pallas_call(
        functools.partial(gather_kernel, planes, held, skip),
        out_shape=tuple(shapes),
        in_specs=[vmem],
        out_specs=(vmem,) * len(shapes),
        scratch_shapes=[pltpu.VMEM(recv.shape, f32)],
        compiler_params=pltpu.CompilerParams(vmem_limit_bytes=VMEM_LIMIT),
        cost_estimate=pl.CostEstimate(flops=int(1e8), bytes_accessed=int(2e6), transcendentals=0),
        name="gather",
    )(recv)


def filter_kernel(
    dims, outer_pieces, inner_piece, grid_ref, outer_ref, inner_ref, from_low_ref, from_high_ref,
    taps_ref, out_ref, mixed, dep,
):
    width, devices, planes = dims
    depth = devices * planes
    outer_count = sum(n for _, n in outer_pieces)
    inner_x, inner_count = inner_piece
    for p in range(planes):
        for c in range(COMPS):
            e = p * COMPS + c
            dep[...] = jnp.zeros(dep.shape, f32)
            off = e * outer_count
            for x, n in outer_pieces:
                dep[pl.ds(x, n), :] = outer_ref[pl.ds(off, n), :]
                off += n
            dep[pl.ds(inner_x, inner_count), :] += inner_ref[pl.ds(e * inner_count, inner_count), :]
            dep[pl.ds(0, 1), :] += from_low_ref[e : e + 1, :].astype(f32)
            dep[pl.ds(width - 1, 1), :] += from_high_ref[e : e + 1, :].astype(f32)
            for j in range(devices):
                lanes = slice(j * LANES, (j + 1) * LANES)
                fluid = grid_ref[pl.ds(c * width * depth + j * planes + p, width, stride=depth), :]
                mixed[pl.ds(e * width, width), lanes] = fluid + dep[0:width, lanes].astype(bf16).astype(f32)
    folds = taps_ref.shape[2]
    block = taps_ref.shape[3]
    sides = []
    for sign in range(2):
        highs, lows = [], []
        for i in range(folds):
            one = mixed[:, i * block : (i + 1) * block]
            two = mixed[:, (i + folds) * block : (i + folds + 1) * block]
            value = one + two if sign == 0 else one - two
            high = value.astype(bf16)
            highs.append(high)
            lows.append((value - high.astype(f32)).astype(bf16))
        sides.append((highs, lows))
    for o in range(folds):
        results = []
        for sign in range(2):
            highs, lows = sides[sign]
            sums = {1: None, -1: None}
            for i in range(folds):
                d = (o - i) % folds
                key = -1 if sign == 1 and o < i else 1
                part = jnp.dot(highs[i], taps_ref[0, sign, d], preferred_element_type=f32)
                part = part + jnp.dot(lows[i], taps_ref[0, sign, d], preferred_element_type=f32)
                part = part + jnp.dot(highs[i], taps_ref[1, sign, d], preferred_element_type=f32)
                sums[key] = part if sums[key] is None else sums[key] + part
            results.append(sums[1] if sums[-1] is None else sums[1] - sums[-1])
        for flip in range(2):
            value = results[0] + results[1] if flip == 0 else results[0] - results[1]
            for half in range(block // LANES):
                j = (o + flip * folds) * (block // LANES) + half
                for p in range(planes):
                    for c in range(COMPS):
                        e = p * COMPS + c
                        out_ref[pl.ds(c * width * depth + j * planes + p, width, stride=depth), :] = value[
                            e * width : (e + 1) * width, half * LANES : (half + 1) * LANES
                        ]


def message_rows(planes, held):
    return -(-(planes * COMPS * held + 2 * planes) // 16) * 16


def exchange(low, high):
    size = lax.axis_size("px")
    even = lax.axis_index("px") % 2 == 0
    first = [(i, i ^ 1) for i in range(size)]
    second = [(i, (i + 1) % size if i % 2 else (i - 1) % size) for i in range(size)]
    far = lax.ppermute(jnp.where(even, low, high), "px", second)
    close = lax.ppermute(jnp.where(even, high, low), "px", first)
    return jnp.where(even, far, close), jnp.where(even, close, far)


def per_device(fluid, part_vel, part_frac, stokes_time, cells, counts):
    devices = lax.axis_size("py")
    _, width, planes, length = fluid.shape
    subs_x, subs_y, slots = stokes_time.shape
    depth = planes * devices
    tile_x = width // subs_x
    params = pltpu.CompilerParams(vmem_limit_bytes=VMEM_LIMIT)
    vmem = pl.BlockSpec(memory_space=pltpu.VMEM)
    dims = (width, devices, planes)

    outer = ((0, tile_x + 1), (width - tile_x - 1, tile_x + 1))
    inner = (tile_x - 1, width - 2 * tile_x + 2)
    outer_count = 2 * (tile_x + 1)
    inner_count = inner[1]
    grid = fluid.reshape(COMPS * width, planes, devices, LANES).transpose(0, 2, 1, 3)
    grid = grid.reshape(COMPS * width * depth, LANES)
    outer_rows = message_rows(planes, outer_count)
    inner_rows = message_rows(planes, inner_count)
    hbm = pl.BlockSpec(memory_space=pltpu.HBM)

    def pack(pieces, total, limit):
        count = sum(n for _, n in pieces)
        return pl.pallas_call(
            functools.partial(pack_kernel, dims, pieces),
            out_shape=jax.ShapeDtypeStruct((devices, total, LANES), bf16),
            in_specs=[hbm],
            out_specs=vmem,
            scratch_shapes=[
                pltpu.VMEM((devices * total, LANES), f32),
                pltpu.VMEM((COMPS * count * depth + 8 * depth, LANES), f32),
                pltpu.SemaphoreType.DMA((COMPS * len(pieces),)),
            ],
            compiler_params=pltpu.CompilerParams(vmem_limit_bytes=limit),
            cost_estimate=pl.CostEstimate(flops=int(1e8), bytes_accessed=int(2e6), transcendentals=0),
            name="pack",
        )(grid)

    send_outer = pack(outer, outer_rows, VMEM_MOST)
    send_inner = pack((inner,), inner_rows, VMEM_MOST)
    recv_outer = lax.all_to_all(send_outer, "py", 0, 0, tiled=True)
    recv_outer, send_inner = lax.optimization_barrier((recv_outer, send_inner))
    recv_inner = lax.all_to_all(send_inner, "py", 0, 0, tiled=True)

    edge_rows = devices * planes * (COMPS + 2)
    low, high = pl.pallas_call(
        functools.partial(edge_kernel, planes, outer_count),
        out_shape=(jax.ShapeDtypeStruct((edge_rows, LANES), bf16),) * 2,
        in_specs=[vmem],
        out_specs=(vmem, vmem),
        scratch_shapes=[pltpu.VMEM((outer_rows, LANES), f32), pltpu.VMEM((2, edge_rows, LANES), f32)],
        compiler_params=params,
        name="edges",
    )(recv_outer)
    before, after = exchange(low, high)

    sizes = (width, devices, planes, subs_x, subs_y, slots, min(256, slots))
    half = tile_x + 1
    outer_plan = (
        outer_count, ((0, half, 1), (half, half, half + 1)), True, (0, tile_x + 2), (0, subs_x - 1), False,
    )
    inner_plan = (inner_count, ((0, inner_count, 0),), False, (0, tile_x), (1, 2), True)
    vel_outer, back_outer = particle_call(
        sizes, outer_plan, counts, recv_outer, part_vel, part_frac, stokes_time, cells, (before, after)
    )
    pencil_outer = lax.all_to_all(back_outer, "py", 0, 0, tiled=True)
    vel_next, back_inner = particle_call(
        sizes, inner_plan, counts, recv_inner, part_vel, part_frac, stokes_time, cells, (vel_outer,)
    )
    pencil_outer, back_inner = lax.optimization_barrier((pencil_outer, back_inner))
    pencil_inner = lax.all_to_all(back_inner, "py", 0, 0, tiled=True)
    dep_outer, low, high = gather_call(planes, outer_count + 2, 1, pencil_outer)
    from_low, from_high = exchange(low, high)
    (dep_inner,) = gather_call(planes, inner_count, 0, pencil_inner)
    taps_high, taps_low = filter_blocks(length, 256)
    out = pl.pallas_call(
        functools.partial(filter_kernel, dims, outer, inner),
        out_shape=jax.ShapeDtypeStruct(grid.shape, f32),
        in_specs=[vmem] * 6,
        out_specs=vmem,
        scratch_shapes=[
            pltpu.VMEM((planes * COMPS * width, length), f32),
            pltpu.VMEM((width + 8, length), f32),
        ],
        compiler_params=params,
        name="filter",
    )(grid, dep_outer, dep_inner, from_low, from_high, jnp.asarray(np.stack([taps_high, taps_low])))
    out = out.reshape(COMPS * width, devices, planes, LANES).transpose(0, 2, 1, 3)
    return out.reshape(fluid.shape), vel_next


def solution(mesh):
    placed = (
        P(None, "px", "py", None),
        P(None, "px", "py", None),
        P(None, "px", "py", None),
        P("px", "py", None),
        P("px", "py", None),
        P("px", "py"),
    )
    return jax.shard_map(
        per_device,
        mesh=mesh,
        in_specs=placed,
        out_specs=(P(None, "px", "py", None), P(None, "px", "py", None)),
        check_vma=False,
    )
```

```python
import functools
import math

import jax
import jax.numpy as jnp
import numpy as np
from jax import lax
from jax.experimental import pallas as pl
from jax.experimental.pallas import tpu as pltpu
from jax.sharding import PartitionSpec as P

mass_load = 4.0
step_dt = 0.5
viscous_step = 0.25
forcing_gain = 1.5
forced_modes = 4

COMPS = 3
LANES = 128
VMEM_LIMIT = 24 * 1024 * 1024
VMEM_MOST = 58 * 1024 * 1024
f32 = jnp.float32
bf16 = jnp.bfloat16
NT = (((1,), (1,)), ((), ()))
NN = (((1,), (0,)), ((), ()))


def filter_blocks(length, width):
    k = np.fft.fftfreq(length, 1.0 / length)
    angle = 2.0 * math.pi * k / length
    gain = np.exp(-viscous_step * angle * angle)
    gain = gain * np.where((abs(k) >= 1) & (abs(k) <= forced_modes), 1.0 + forcing_gain, 1.0)
    taps = np.fft.ifft(gain).real
    blocks = length // width
    half = blocks // 2
    inner = np.arange(width)
    full = []
    for d in range(blocks):
        full.append(taps[(width * d + inner[None, :] - inner[:, None]) % length])
    sums = np.stack([0.5 * (full[d] + full[d + half]) for d in range(half)])
    diffs = np.stack([0.5 * (full[d] - full[d + half]) for d in range(half)])
    both = np.stack([sums, diffs]).astype(np.float32)
    high = both.astype(jnp.bfloat16)
    low = (both - high.astype(np.float32)).astype(jnp.bfloat16)
    return high, low


def side_picker():
    row_id = lax.broadcasted_iota(jnp.int32, (8, LANES), 0)
    lane_id = lax.broadcasted_iota(jnp.int32, (8, LANES), 1)
    pick = ((row_id == 0) & (lane_id == LANES - 1)) | ((row_id == 1) & (lane_id == 0))
    return jnp.where(pick, 1.0, 0.0).astype(bf16)


def pack_kernel(dims, pieces, grid_hbm, out_ref, msg, held, sems):
    width, devices, planes = dims
    depth = devices * planes
    count = sum(n for _, n in pieces)
    rows = COMPS * count
    used = planes * rows
    total = out_ref.shape[1]
    copies = []
    for c in range(COMPS):
        off = c * count
        for x, n in pieces:
            copy = pltpu.make_async_copy(
                grid_hbm.at[pl.ds((c * width + x) * depth, n * depth), :],
                held.at[pl.ds(off * depth, n * depth), :],
                sems.at[len(copies)],
            )
            copy.start()
            copies.append(copy)
            off += n
    pick = side_picker()
    for j in range(devices):
        msg[pl.ds(j * total + used, total - used), :] = jnp.zeros((total - used, LANES), f32)
    for c in range(COMPS):
        for i in range(len(pieces)):
            copies[c * len(pieces) + i].wait()
        for j in range(devices):
            for p in range(planes):
                msg[pl.ds(j * total + p * rows + c * count, count), :] = held[
                    pl.ds(c * count * depth + j * planes + p, count, stride=depth), :
                ]
    for j in range(devices):
        for p in range(planes):
            block = msg[pl.ds(j * total + p * rows, rows), :].astype(bf16)
            edge = lax.dot_general(pick, block, NT, preferred_element_type=f32)
            right = (j + 1) % devices
            left = (j - 1) % devices
            msg[pl.ds(right * total + used + 2 * p, 1), 0:rows] = edge[0:1]
            msg[pl.ds(left * total + used + 2 * p + 1, 1), 0:rows] = edge[1:2]
    for j in range(devices):
        out_ref[j] = msg[pl.ds(j * total, total), :].astype(bf16)


def edge_kernel(planes, count, recv_ref, low_ref, high_ref, msg, out):
    devices = recv_ref.shape[0]
    used = planes * COMPS * count
    lines = planes * COMPS
    for s in range(devices):
        msg[...] = recv_ref[s].astype(f32)
        for e in range(lines):
            for side in range(2):
                at = e * count + side * (count - 1)
                out[side, pl.ds(s * lines + e, 1), :] = msg[pl.ds(at, 1), :]
        for side in range(2):
            out[side, pl.ds(devices * lines + s * 2 * planes, 2 * planes), :] = msg[pl.ds(used, 2 * planes), :]
    low_ref[...] = out[0].astype(bf16)
    high_ref[...] = out[1].astype(bf16)


def lane_of_x(local, c, count, ghosts):
    if not ghosts:
        return c * count + local
    lane = c * count + local - 1
    lane = jnp.where(local == 0, LANES // 2 + c * count + count - 1, lane)
    return jnp.where(local == count + 1, LANES // 2 + c * count, lane)


def same_cell(c, count, ghosts, depth, rows):
    local = lax.broadcasted_iota(jnp.int32, (rows, LANES), 0) // depth
    col = lax.broadcasted_iota(jnp.int32, (rows, LANES), 1)
    return jnp.where(col == lane_of_x(local, c, count, ghosts), 1.0, 0.0).astype(bf16)


def side_lane(depth, shape, dim):
    ghost = lax.broadcasted_iota(jnp.int32, shape, dim)
    lane = lax.broadcasted_iota(jnp.int32, shape, 1 - dim)
    hit = ((ghost < depth) & (lane == LANES - 1)) | ((ghost >= depth) & (lane == 0))
    return jnp.where(hit, 1.0, 0.0).astype(bf16)


def particle_kernel(dims, plan, *refs):
    width, devices, planes, subs_x, subs_y, slots, chunk = dims
    count, moves, ghosts, starts, strips, writes_all = plan
    counts_ref, recv_ref, vel_ref, frac_ref, tau_ref, cells_ref = refs[:6]
    refs = refs[6:]
    if ghosts:
        before_ref, after_ref = refs[:2]
        refs = refs[2:]
    if writes_all:
        other_ref = refs[0]
        refs = refs[1:]
    vel_out_ref, send_ref, msg, rows_buf, ghost, field, deposit, prep, ints = refs
    held = count + 2 if ghosts else count
    depth = devices * planes
    tile_x = width // subs_x
    tile_y = LANES // subs_y
    total = recv_ref.shape[1]
    rows = COMPS * count
    used = planes * rows
    cells = held * depth
    near = 4
    pair = 2 * depth
    pairs = tile_x // 2
    strip_rows = tile_x * depth
    core = len(starts) * strip_rows
    block = near * depth

    if writes_all:
        others = [a for a in range(subs_x) if a not in strips]
        for c in range(COMPS):
            for i, a in enumerate(others):
                vel_out_ref[c, a] = other_ref[c, i]

    lines = planes * COMPS
    for s in range(devices):
        msg[pl.ds(0, total), :] = recv_ref[s].astype(f32)
        for p in range(planes):
            z = s * planes + p
            for c in range(COMPS):
                for off, n, local in moves:
                    rows_buf[pl.ds(c * cells + local * depth + z, n, stride=depth), :] = msg[
                        pl.ds(p * rows + c * count + off, n), :
                    ]
            ghost[pl.ds(z, 1), :] = msg[pl.ds(used + 2 * p, 1), :]
            ghost[pl.ds(depth + z, 1), :] = msg[pl.ds(used + 2 * p + 1, 1), :]
    if ghosts:
        lane8 = lax.broadcasted_iota(jnp.int32, (2 * depth, LANES), 1)
        for side, ref in enumerate((before_ref, after_ref)):
            msg[pl.ds(0, ref.shape[0]), :] = ref[...].astype(f32)
            for s in range(devices):
                for p in range(planes):
                    z = s * planes + p
                    for c in range(COMPS):
                        at = c * cells + side * (held - 1) * depth + z
                        rows_buf[pl.ds(at, 1), :] = msg[pl.ds(s * lines + p * COMPS + c, 1), :]
            turned = []
            for lr in range(2):
                turned.append(msg[pl.ds(devices * lines + lr, depth, stride=2), :])
            turned = jnp.roll(jnp.concatenate(turned, axis=0), LANES // 2, axis=1)
            wanted = (lane8 - LANES // 2) % count == (count - 1 if side == 0 else 0)
            ghost[...] = jnp.where((lane8 >= LANES // 2) & wanted, turned, ghost[...])
    own_z = lax.broadcasted_iota(jnp.int32, (cells, 2 * depth), 0) % depth
    own_z = own_z == lax.broadcasted_iota(jnp.int32, (cells, 2 * depth), 1) % depth
    lane = lax.broadcasted_iota(jnp.int32, (cells, LANES), 1)
    strip_lane = lane[:strip_rows]
    for c in range(COMPS):
        at = pl.ds(c * cells, cells)
        wide = lax.dot_general(
            same_cell(c, count, ghosts, depth, cells), ghost[...].astype(bf16), NT, preferred_element_type=f32
        )
        wide = jnp.where(own_z, wide, 0.0).astype(bf16)
        outer = jnp.dot(wide, side_lane(depth, (2 * depth, LANES), 0), preferred_element_type=f32)
        inner = rows_buf[at, :]
        lower = jnp.where(lane == LANES - 1, outer, inner)
        upper = jnp.where(lane == 0, outer, inner)
        for side, value in enumerate((lower, upper)):
            moved = jnp.roll(value, LANES // 2, axis=1)
            for b in range(side * subs_y // 2, (side + 1) * subs_y // 2):
                first_half = (strip_lane - (b * tile_y - 16)) % LANES < LANES // 2
                for k, start in enumerate(starts):
                    r = start * depth
                    field[b, pl.ds(c * core + k * strip_rows, strip_rows), :] = jnp.where(
                        first_half, value[r : r + strip_rows], moved[r + pair : r + pair + strip_rows]
                    ).astype(bf16)

    x_rows = lax.broadcasted_iota(jnp.int32, (8, chunk), 0)
    z_rows = lax.broadcasted_iota(jnp.int32, (depth, chunk), 0)
    y_rows = lax.broadcasted_iota(jnp.int32, (tile_y + 16, chunk), 0) - 8

    def strip(k, carry):
        a = strips[0] + k * (strips[1] - strips[0])
        place_a = k if not writes_all else a
        for d in range(COMPS):
            f = frac_ref[d, a]
            prep[3 * d] = 0.5 * (0.5 - f) ** 2
            prep[3 * d + 1] = 0.75 - f * f
            prep[3 * d + 2] = 0.5 * (0.5 + f) ** 2
        prep[9] = step_dt / tau_ref[a]
        cell = cells_ref[a]
        ints[0] = cell // (tile_y * depth)
        ints[1] = cell // depth % tile_y
        ints[2] = cell % depth
        first = k * strip_rows

        for b in range(subs_y):
            filled = counts_ref[a, b]
            blocks = tile_x * depth // block
            data = jnp.concatenate(
                [
                    jnp.concatenate(
                        [
                            field[b, pl.ds(pl.multiple_of(c * core + first + t * block, block), block), :]
                            for t in range(blocks)
                        ],
                        axis=1,
                    )
                    for c in range(COMPS)
                ],
                axis=0,
            )
            acc = None
            for start in range(0, slots, chunk):
                at = slice(start, start + chunk)
                row = lambda i: prep[i, b : b + 1, at]
                xc, yc, zc = (ints[i, b : b + 1, at] for i in range(3))
                here = lax.broadcasted_iota(jnp.int32, (1, chunk), 1) + start < filled
                dx = x_rows - (xc & 1)
                wx = jnp.where(
                    dx == 0, row(0), jnp.where(dx == 1, row(1), jnp.where(dx == 2, row(2), 0.0))
                )
                dy = y_rows - yc
                y_low, y_mid, y_high = (jnp.where(here, row(3 + i), 0.0) for i in range(3))
                wy = jnp.where(
                    dy == -1, y_low, jnp.where(dy == 0, y_mid, jnp.where(dy == 1, y_high, 0.0))
                )
                dz = (z_rows - zc + 1) & (depth - 1)
                wz = jnp.where(
                    dz == 0, row(6), jnp.where(dz == 1, row(7), jnp.where(dz == 2, row(8), 0.0))
                )
                groups = LANES // 8
                half_groups = groups // 2
                blank = jnp.zeros((8, chunk), f32)
                pieces = [blank] * (groups * blocks)
                for q in range(pairs):
                    chosen = xc >> 1 == q
                    for g in range(tile_y // 8 + 2):
                        place = (b * tile_y // 8 - 1 + g + (q % 2) * half_groups) % groups
                        pieces[q // 2 * groups + place] = jnp.where(chosen, wy[8 * g : 8 * g + 8], 0.0)
                wy = jnp.concatenate(pieces, axis=0).astype(bf16)
                raw = jnp.dot(data, wy, preferred_element_type=f32)
                rate = row(9)
                shares = []
                for c in range(COMPS):
                    found = None
                    for i in range(near):
                        part = None
                        for g in range(depth // 8):
                            at8 = c * block + i * depth + 8 * g
                            term = raw[at8 : at8 + 8] * wz[8 * g : 8 * g + 8]
                            part = term if part is None else part + term
                        part = part * wx[i : i + 1]
                        found = part if found is None else found + part
                    interp = jnp.sum(found, axis=0, keepdims=True)
                    velocity = vel_ref[c, a, b : b + 1, at]
                    change = rate * (interp - velocity)
                    vel_out_ref[c, place_a, b : b + 1, at] = jnp.where(here, velocity + change, velocity)
                    pull = jnp.where(here, -mass_load * change, 0.0) * wx
                    shares = shares + [(pull[i : i + 1] * wz).astype(bf16) for i in range(near)]
                part = lax.dot_general(
                    jnp.concatenate(shares, axis=0), wy, NT, preferred_element_type=f32
                )
                acc = part if acc is None else acc + part
            for c in range(COMPS):
                for t in range(blocks):
                    base = pl.multiple_of(c * core + first + t * block, block)
                    deposit[b, pl.ds(base, block), :] = acc[
                        c * block : (c + 1) * block, t * LANES : (t + 1) * LANES
                    ]
        return carry

    lax.fori_loop(0, len(strips), strip, 0)

    gathered = jnp.zeros((2 * depth, LANES), f32)
    empty = jnp.zeros((pair, LANES), f32)
    for c in range(COMPS):
        at = pl.ds(c * cells, cells)
        sides = []
        for side in range(2):
            found = []
            for k in range(len(starts)):
                even = odd = None
                for b in range(side * subs_y // 2, (side + 1) * subs_y // 2):
                    value = deposit[b, pl.ds(c * core + k * strip_rows, strip_rows), :]
                    first_half = (strip_lane - (b * tile_y - 16)) % LANES < LANES // 2
                    one = jnp.where(first_half, value, 0.0)
                    two = jnp.where(first_half, 0.0, value)
                    even = one if even is None else even + one
                    odd = two if odd is None else odd + two
                moved = jnp.roll(odd, LANES // 2, axis=1)
                found.append(
                    jnp.concatenate([even, empty], axis=0) + jnp.concatenate([empty, moved], axis=0)
                )
            shared = strip_rows + pair - (starts[1] - starts[0]) * depth
            if shared == 0:
                sides.append(jnp.concatenate(found, axis=0))
            else:
                keep = strip_rows + pair - shared
                middle = found[0][keep:] + found[1][:shared]
                sides.append(jnp.concatenate([found[0][:keep], middle, found[1][shared:]], axis=0))
        lower, upper = sides
        first_lane = lane == 0
        last_lane = lane == LANES - 1
        rows_buf[at, :] = jnp.where(last_lane, 0.0, lower) + jnp.where(first_lane, 0.0, upper)
        outer = jnp.where(last_lane, lower, jnp.where(first_lane, upper, 0.0)).astype(bf16)
        wide = jnp.dot(outer, side_lane(depth, (LANES, 2 * depth), 1), preferred_element_type=f32)
        wide = jnp.where(own_z, wide, 0.0).astype(bf16)
        gathered = gathered + lax.dot_general(
            wide, same_cell(c, held, False, depth, cells), (((0,), (0,)), ((), ())), preferred_element_type=f32
        )
    ghost[...] = gathered
    rows = COMPS * held
    used = planes * rows
    total = send_ref.shape[1]
    for s in range(devices):
        if total > used + 2 * planes:
            msg[pl.ds(used, total - used), :] = jnp.zeros((total - used, LANES), f32)
        for p in range(planes):
            z = s * planes + p
            for c in range(COMPS):
                msg[pl.ds(p * rows + c * held, held), :] = rows_buf[
                    pl.ds(c * cells + z, held, stride=depth), :
                ]
            msg[pl.ds(used + 2 * p, 1), :] = ghost[pl.ds(z, 1), :]
            msg[pl.ds(used + 2 * p + 1, 1), :] = ghost[pl.ds(depth + z, 1), :]
        send_ref[s] = msg[pl.ds(0, total), :].astype(bf16)


def particle_call(dims, plan, counts, recv, part_vel, part_frac, stokes_time, cells, extra):
    width, devices, planes, subs_x, subs_y, slots, chunk = dims
    count, moves, ghosts, starts, strips, writes_all = plan
    vmem = pl.BlockSpec(memory_space=pltpu.VMEM)
    held = count + 2 if ghosts else count
    depth = devices * planes
    total_out = message_rows(planes, held)
    core_rows = COMPS * len(strips) * (width // subs_x) * depth
    vel_shape = part_vel.shape if writes_all else (COMPS, len(strips), subs_y, slots)
    return pl.pallas_call(
        functools.partial(particle_kernel, dims, plan),
        out_shape=(
            jax.ShapeDtypeStruct(vel_shape, f32),
            jax.ShapeDtypeStruct((devices, total_out, LANES), bf16),
        ),
        in_specs=[pl.BlockSpec(memory_space=pltpu.SMEM)] + [vmem] * (5 + len(extra)),
        out_specs=(vmem, vmem),
        scratch_shapes=[
            pltpu.VMEM((devices * planes * 5, LANES), f32),
            pltpu.VMEM((COMPS * held * depth + 8 * depth, LANES), f32),
            pltpu.VMEM((2 * depth, LANES), f32),
            pltpu.VMEM((subs_y, core_rows, LANES), bf16),
            pltpu.VMEM((subs_y, core_rows, LANES), f32),
            pltpu.VMEM((10, subs_y, slots), f32),
            pltpu.VMEM((3, subs_y, slots), jnp.int32),
        ],
        compiler_params=pltpu.CompilerParams(vmem_limit_bytes=VMEM_LIMIT),
        cost_estimate=pl.CostEstimate(flops=int(8e9), bytes_accessed=int(2e7), transcendentals=0),
        name="particles_outer" if ghosts else "particles_inner",
    )(counts, recv, part_vel, part_frac, stokes_time, cells, *extra)


def gather_kernel(planes, held, skip, recv_ref, out_ref, *refs):
    msg = refs[-1]
    rows = COMPS * held
    used = planes * rows
    count = recv_ref.shape[0]
    inner = held - 2 * skip
    for j in range(count):
        msg[j] = recv_ref[j].astype(f32)
    place = side_picker()
    for j in range(count):
        left = (j - 1) % count
        right = (j + 1) % count
        lanes = slice(j * LANES, (j + 1) * LANES)
        lows, highs = [], []
        for p in range(planes):
            pair = jnp.concatenate(
                [
                    msg[right, used + 2 * p : used + 2 * p + 1, :],
                    msg[left, used + 2 * p + 1 : used + 2 * p + 2, :],
                    jnp.zeros((6, LANES), f32),
                ],
                axis=0,
            ).astype(bf16)
            added = lax.dot_general(
                pair, place, (((0,), (0,)), ((), ())), preferred_element_type=f32
            )
            block = msg[j, p * rows : (p + 1) * rows, :] + added[:rows]
            for c in range(COMPS):
                e = p * COMPS + c
                at = c * held
                lows.append(block[at : at + 1])
                highs.append(block[at + held - 1 : at + held])
                out_ref[pl.ds(e * inner, inner), lanes] = block[at + skip : at + skip + inner]
        if skip:
            refs[0][:, lanes] = jnp.concatenate(lows, axis=0).astype(bf16)
            refs[1][:, lanes] = jnp.concatenate(highs, axis=0).astype(bf16)


def gather_call(planes, held, skip, recv):
    devices = recv.shape[0]
    length = devices * LANES
    vmem = pl.BlockSpec(memory_space=pltpu.VMEM)
    lines = planes * COMPS
    shapes = [jax.ShapeDtypeStruct((lines * (held - 2 * skip), length), f32)]
    if skip:
        shapes += [jax.ShapeDtypeStruct((lines, length), bf16)] * 2
    return pl.pallas_call(
        functools.partial(gather_kernel, planes, held, skip),
        out_shape=tuple(shapes),
        in_specs=[vmem],
        out_specs=(vmem,) * len(shapes),
        scratch_shapes=[pltpu.VMEM(recv.shape, f32)],
        compiler_params=pltpu.CompilerParams(vmem_limit_bytes=VMEM_LIMIT),
        cost_estimate=pl.CostEstimate(flops=int(1e8), bytes_accessed=int(2e6), transcendentals=0),
        name="gather",
    )(recv)


def filter_kernel(
    dims, outer_pieces, inner_piece, grid_ref, outer_ref, inner_ref, from_low_ref, from_high_ref,
    taps_ref, out_ref, mixed, dep,
):
    width, devices, planes = dims
    depth = devices * planes
    outer_count = sum(n for _, n in outer_pieces)
    inner_x, inner_count = inner_piece
    for p in range(planes):
        for c in range(COMPS):
            e = p * COMPS + c
            dep[...] = jnp.zeros(dep.shape, f32)
            off = e * outer_count
            for x, n in outer_pieces:
                dep[pl.ds(x, n), :] = outer_ref[pl.ds(off, n), :]
                off += n
            dep[pl.ds(inner_x, inner_count), :] += inner_ref[pl.ds(e * inner_count, inner_count), :]
            dep[pl.ds(0, 1), :] += from_low_ref[e : e + 1, :].astype(f32)
            dep[pl.ds(width - 1, 1), :] += from_high_ref[e : e + 1, :].astype(f32)
            for j in range(devices):
                lanes = slice(j * LANES, (j + 1) * LANES)
                fluid = grid_ref[pl.ds(c * width * depth + j * planes + p, width, stride=depth), :]
                mixed[pl.ds(e * width, width), lanes] = fluid + dep[0:width, lanes].astype(bf16).astype(f32)
    block = taps_ref.shape[3]
    folds = mixed.shape[1] // block // 2
    sides = []
    for sign in range(2):
        highs, lows = [], []
        for i in range(folds):
            one = mixed[:, i * block : (i + 1) * block]
            two = mixed[:, (i + folds) * block : (i + folds + 1) * block]
            value = one + two if sign == 0 else one - two
            high = value.astype(bf16)
            highs.append(high)
            lows.append((value - high.astype(f32)).astype(bf16))
        sides.append((highs, lows))
    for o in range(folds):
        results = []
        for sign in range(2):
            highs, lows = sides[sign]
            sums = {1: None, -1: None}
            for i in range(folds):
                d = (o - i) % folds
                key = -1 if sign == 1 and o < i else 1
                kind = NN
                if d > folds // 2:
                    d, kind = folds - d, NT
                    key = -key if sign == 1 else key
                high, low = taps_ref[0, sign, d], taps_ref[1, sign, d]
                part = lax.dot_general(highs[i], high, kind, preferred_element_type=f32)
                part = part + lax.dot_general(lows[i], high, kind, preferred_element_type=f32)
                part = part + lax.dot_general(highs[i], low, kind, preferred_element_type=f32)
                sums[key] = part if sums[key] is None else sums[key] + part
            results.append(sums[1] if sums[-1] is None else sums[1] - sums[-1])
        for flip in range(2):
            value = results[0] + results[1] if flip == 0 else results[0] - results[1]
            for half in range(block // LANES):
                j = (o + flip * folds) * (block // LANES) + half
                for p in range(planes):
                    for c in range(COMPS):
                        e = p * COMPS + c
                        out_ref[pl.ds(c * width * depth + j * planes + p, width, stride=depth), :] = value[
                            e * width : (e + 1) * width, half * LANES : (half + 1) * LANES
                        ]


def message_rows(planes, held):
    return -(-(planes * COMPS * held + 2 * planes) // 16) * 16


def exchange(low, high):
    size = lax.axis_size("px")
    even = lax.axis_index("px") % 2 == 0
    first = [(i, i ^ 1) for i in range(size)]
    second = [(i, (i + 1) % size if i % 2 else (i - 1) % size) for i in range(size)]
    far = lax.ppermute(jnp.where(even, low, high), "px", second)
    close = lax.ppermute(jnp.where(even, high, low), "px", first)
    return jnp.where(even, far, close), jnp.where(even, close, far)


def per_device(fluid, part_vel, part_frac, stokes_time, cells, counts):
    devices = lax.axis_size("py")
    _, width, planes, length = fluid.shape
    subs_x, subs_y, slots = stokes_time.shape
    depth = planes * devices
    tile_x = width // subs_x
    params = pltpu.CompilerParams(vmem_limit_bytes=VMEM_LIMIT)
    vmem = pl.BlockSpec(memory_space=pltpu.VMEM)
    dims = (width, devices, planes)

    outer = ((0, tile_x + 1), (width - tile_x - 1, tile_x + 1))
    inner = (tile_x - 1, width - 2 * tile_x + 2)
    outer_count = 2 * (tile_x + 1)
    inner_count = inner[1]
    grid = fluid.reshape(COMPS * width, planes, devices, LANES).transpose(0, 2, 1, 3)
    grid = grid.reshape(COMPS * width * depth, LANES)
    outer_rows = message_rows(planes, outer_count)
    inner_rows = message_rows(planes, inner_count)
    hbm = pl.BlockSpec(memory_space=pltpu.HBM)

    def pack(pieces, total, limit):
        count = sum(n for _, n in pieces)
        return pl.pallas_call(
            functools.partial(pack_kernel, dims, pieces),
            out_shape=jax.ShapeDtypeStruct((devices, total, LANES), bf16),
            in_specs=[hbm],
            out_specs=vmem,
            scratch_shapes=[
                pltpu.VMEM((devices * total, LANES), f32),
                pltpu.VMEM((COMPS * count * depth + 8 * depth, LANES), f32),
                pltpu.SemaphoreType.DMA((COMPS * len(pieces),)),
            ],
            compiler_params=pltpu.CompilerParams(vmem_limit_bytes=limit),
            cost_estimate=pl.CostEstimate(flops=int(1e8), bytes_accessed=int(2e6), transcendentals=0),
            name="pack",
        )(grid)

    send_outer = pack(outer, outer_rows, VMEM_MOST)
    send_inner = pack((inner,), inner_rows, VMEM_MOST)
    recv_outer = lax.all_to_all(send_outer, "py", 0, 0, tiled=True)
    recv_outer, send_inner = lax.optimization_barrier((recv_outer, send_inner))
    recv_inner = lax.all_to_all(send_inner, "py", 0, 0, tiled=True)

    edge_rows = devices * planes * (COMPS + 2)
    low, high = pl.pallas_call(
        functools.partial(edge_kernel, planes, outer_count),
        out_shape=(jax.ShapeDtypeStruct((edge_rows, LANES), bf16),) * 2,
        in_specs=[vmem],
        out_specs=(vmem, vmem),
        scratch_shapes=[pltpu.VMEM((outer_rows, LANES), f32), pltpu.VMEM((2, edge_rows, LANES), f32)],
        compiler_params=params,
        name="edges",
    )(recv_outer)
    before, after = exchange(low, high)

    sizes = (width, devices, planes, subs_x, subs_y, slots, min(256, slots))
    half = tile_x + 1
    outer_plan = (
        outer_count, ((0, half, 1), (half, half, half + 1)), True, (0, tile_x + 2), (0, subs_x - 1), False,
    )
    inner_plan = (inner_count, ((0, inner_count, 0),), False, (0, tile_x), (1, 2), True)
    vel_outer, back_outer = particle_call(
        sizes, outer_plan, counts, recv_outer, part_vel, part_frac, stokes_time, cells, (before, after)
    )
    pencil_outer = lax.all_to_all(back_outer, "py", 0, 0, tiled=True)
    vel_next, back_inner = particle_call(
        sizes, inner_plan, counts, recv_inner, part_vel, part_frac, stokes_time, cells, (vel_outer,)
    )
    pencil_outer, back_inner = lax.optimization_barrier((pencil_outer, back_inner))
    pencil_inner = lax.all_to_all(back_inner, "py", 0, 0, tiled=True)
    dep_outer, low, high = gather_call(planes, outer_count + 2, 1, pencil_outer)
    from_low, from_high = exchange(low, high)
    (dep_inner,) = gather_call(planes, inner_count, 0, pencil_inner)
    taps_high, taps_low = filter_blocks(length, 256)
    out = pl.pallas_call(
        functools.partial(filter_kernel, dims, outer, inner),
        out_shape=jax.ShapeDtypeStruct(grid.shape, f32),
        in_specs=[vmem] * 6,
        out_specs=vmem,
        scratch_shapes=[
            pltpu.VMEM((planes * COMPS * width, length), f32),
            pltpu.VMEM((width + 8, length), f32),
        ],
        compiler_params=params,
        name="filter",
    )(grid, dep_outer, dep_inner, from_low, from_high, jnp.asarray(np.stack([taps_high, taps_low])[:, :, : length // 1024 + 1]))
    out = out.reshape(COMPS * width, devices, planes, LANES).transpose(0, 2, 1, 3)
    return out.reshape(fluid.shape), vel_next


def solution(mesh):
    placed = (
        P(None, "px", "py", None),
        P(None, "px", "py", None),
        P(None, "px", "py", None),
        P("px", "py", None),
        P("px", "py", None),
        P("px", "py"),
    )
    return jax.shard_map(
        per_device,
        mesh=mesh,
        in_specs=placed,
        out_specs=(P(None, "px", "py", None), P(None, "px", "py", None)),
        check_vma=False,
    )
```
